512 devices in a mesh: ctx: 16 (over z), batch: 8 (over y, core), mp: 4 (over x).
Axes of the slice: x: 4, y: 4, z: 16, core: 2. Of those that a mesh axis runs over, the one named last changes fastest.
Arguments:
- kv_cache: bfloat16 [2, 16, 16384, 4, 128], P(None, 'batch', 'ctx', 'mp'), may hold values from -6 to 6
- backup_codes: bfloat16 [2, 16, 16384, 4, 128], P(None, 'batch', 'ctx', 'mp'), may hold values from -6 to 6
- backup_scales: bfloat16 [2, 16, 128, 4], P(None, 'batch', 'ctx', 'mp'), may hold values from 0.5 to 2
- block_shift: int32 [8], replicated, may hold values from 1 to 15, as said below
- failed: int32 [1], replicated, may hold values from 0 to 511
- new_lengths: int32 [16, 15], P('batch'), may hold values from 960 to 1216, as said below
- queries: bfloat16 [16, 4, 64, 128], P('batch', None, 'mp'), may hold values from -32 to 32
- new_kv: bfloat16 [2, 16, 4, 4, 128], P(None, 'batch', None, 'mp'), may hold values from -5 to 5
Outputs:
- new_cache: bfloat16 [2, 16, 19456, 4, 128], P(None, 'batch', 'ctx', 'mp')
- attended: bfloat16 [16, 4, 64, 128], P('batch', None, 'mp')
- log_total: float32 [16, 4, 64], P('batch', None, 'mp')
The draws below stay inside these ranges and needn't reach their ends.
Inputs may be any that keep to these rules, and one draw needn't show every extreme that they name: `new_lengths`: for every sequence the 15 lengths sum to 16384; new shard j begins at or after j * 1024 and ends at or before (j + 2) * 1024; every sequence has a shard of exactly 1216 positions. `block_shift`: some block is held at distance 1, another at distance 16 - 1, another at half the ctx length.
All inputs are finite; a program needn't handle non-finite values.
Results may differ from the reference program's by a relative error of at most 0.0079.
Values may be sent and summed in bfloat16 or wider, within the bound.
A program may use at most 64 MiB of HBM per device.

```python
import math
import jax
import jax.numpy as jnp
from jax import lax

KVH = 4
HD = 128
QH = 64
CTX_DEV = 1024
STEPS = 4
BLK = 128
SEQS = 16
SEQ_LEN = 16384
NB = 8
GAP = 64
CAP = 1216
NEW_SHARDS = 15
GROUP = 16
N_CTX = 16
N_BATCH = 8
DEVICES = 512


def draw_queries(key, part):
    key = jax.random.fold_in(key, 11)
    base_key = jax.random.fold_in(key, 0)
    values = jnp.clip(2.5 * jax.random.normal(base_key, (SEQS, STEPS, QH, HD)), -10.0, 10.0)
    return values.astype(jnp.bfloat16)


def draw_new_kv(key, part):
    key = jax.random.fold_in(key, 23)
    entries = jnp.clip(jax.random.normal(key, (2, SEQS, STEPS, KVH, HD)), -5.0, 5.0)
    return entries.astype(jnp.bfloat16)


def draw_new_lengths(key, part):
    key = jax.random.fold_in(key, 31)
    wobble_key, peak_key = jax.random.split(key)
    wobble = jax.random.randint(wobble_key, (SEQS, NEW_SHARDS + 1), -GAP, GAP + 1)
    peak = jax.random.randint(peak_key, (SEQS, 1), 1, NEW_SHARDS)
    marks = jnp.arange(NEW_SHARDS + 1)[None, :]
    wobble = jnp.where(marks == peak, -GAP, wobble)
    wobble = jnp.where(marks == peak + 1, GAP, wobble)
    wobble = jnp.where(marks == 0, 0, wobble)
    wobble = jnp.where(marks == NEW_SHARDS, GAP, wobble)
    bounds = marks * (CTX_DEV + GAP) + wobble
    return (bounds[:, 1:] - bounds[:, :-1]).astype(jnp.int32)


def draw_block_shift(key, part):
    key = jax.random.fold_in(key, 41)
    shift_key, order_key = jax.random.split(key)
    shifts = jax.random.randint(shift_key, (NB,), 1, N_CTX)
    order = jax.random.permutation(order_key, NB)
    shifts = jnp.where(order == 0, 1, shifts)
    shifts = jnp.where(order == 1, N_CTX - 1, shifts)
    shifts = jnp.where(order == 2, N_CTX // 2, shifts)
    return shifts.astype(jnp.int32)


def block_scale(key, extent, pieces, smallest, high):
    def one(axis_at, shards_of):
        steps = jax.random.uniform(jax.random.fold_in(jax.random.fold_in(key, 6), axis_at), (shards_of,), jnp.float32, smallest / len(pieces), high / len(pieces))
        return jnp.repeat(jnp.exp(steps), extent[axis_at] // shards_of).reshape((-1,) + (1,) * (len(extent) - axis_at - 1))

    factor_of = one(*pieces[0])
    for cut in pieces[1:]:
        factor_of = factor_of * one(*cut)
    return factor_of


def gaussian(stream_key, dims, scale, limit, pieces=(), held_as=jnp.bfloat16):
    drawn = scale * jax.random.normal(stream_key, dims, jnp.float32)
    if pieces:
        drawn = drawn * block_scale(stream_key, dims, pieces, -0.22, 0.18)
    return jnp.clip(drawn, -limit, limit).astype(held_as)


def setup_inputs(seed: int = 0) -> dict:
    seeds = jax.random.split(jax.random.key(seed), 9)
    kv_cache = gaussian(seeds[0], (2, SEQS, SEQ_LEN, KVH, HD), 1.0, 6.0, ((1, 8), (2, 16), (3, 4)))
    backup_codes = gaussian(seeds[1], (2, SEQS, SEQ_LEN, KVH, HD), 1.0, 6.0, ((1, 8), (2, 16), (3, 4)))
    backup_scales = jnp.clip(jnp.exp(math.log(2.0) - 1.3862944 * jax.random.uniform(seeds[2], (2, SEQS, N_CTX * NB, KVH), jnp.float32) ** block_scale(seeds[2], (2, SEQS, N_CTX * NB, KVH), ((1, 8), (2, 16), (3, 4)), -0.2, 0.2)), 0.5, 2.0).astype(jnp.bfloat16)
    block_shift = draw_block_shift(jax.random.fold_in(seeds[8], 71), 0)
    failed = jax.random.randint(seeds[4], (1,), 0, DEVICES).astype(jnp.int32)
    new_lengths = draw_new_lengths(jax.random.fold_in(seeds[8], 71), 0)
    queries = draw_queries(jax.random.fold_in(seeds[8], 71), 0)
    new_kv = draw_new_kv(jax.random.fold_in(seeds[8], 71), 0)
    return dict(kv_cache=kv_cache, backup_codes=backup_codes, backup_scales=backup_scales, block_shift=block_shift, failed=failed, new_lengths=new_lengths, queries=queries, new_kv=new_kv)


def parity_sign(left_ids, right_ids, bit_count):
    shared = jnp.bitwise_and(left_ids[:, None], right_ids[None, :])
    ones_count = jnp.zeros(shared.shape, jnp.int32)
    for bit_pos in range(bit_count):
        ones_count = ones_count + jnp.bitwise_and(jnp.right_shift(shared, bit_pos), 1)
    return (1 - 2 * (ones_count % 2)).astype(jnp.float32)

def reference(kv_cache, backup_codes, backup_scales, block_shift, failed, new_lengths, queries, new_kv):
    seqs_group = SEQS // N_BATCH
    block_count = CTX_DEV // BLK
    failed_ctx = (failed[0] % N_CTX).astype(jnp.int32)
    holders = ((failed_ctx + block_shift) % N_CTX).astype(jnp.int32)
    block_ids = jnp.arange(block_count, dtype=jnp.int32)
    positions = (holders[:, None] * CTX_DEV + block_ids[:, None] * BLK + jnp.arange(BLK, dtype=jnp.int32)[None, :]).reshape(-1).astype(jnp.int32)
    group_codes = jnp.roll(backup_codes, -seqs_group, axis=1)
    lost_codes = jnp.take(group_codes, positions, axis=2)
    group_scales = jnp.roll(backup_scales, -seqs_group, axis=1)
    lost_scales = jnp.take(group_scales, (holders * block_count + block_ids).astype(jnp.int32), axis=2)
    head_table = parity_sign(jnp.arange(HD, dtype=jnp.int32), jnp.arange(HD, dtype=jnp.int32), HD.bit_length())
    turned = jnp.einsum('abtkd,de->abtke', lost_codes.astype(jnp.float32), head_table, precision=lax.Precision.HIGHEST)
    turned = turned.reshape(2, SEQS, block_count, BLK, KVH, HD) * lost_scales.astype(jnp.float32)[:, :, :, None, :, None]
    mix_table = parity_sign(jnp.arange(KVH, dtype=jnp.int32), jnp.arange(KVH, dtype=jnp.int32), KVH.bit_length()) / math.sqrt(KVH * HD)
    restored = jnp.einsum('abnikd,kj->abnijd', turned, mix_table, precision=lax.Precision.HIGHEST)
    restored = restored.reshape(2, SEQS, CTX_DEV, KVH, HD).astype(jnp.bfloat16)
    zero_index = jnp.zeros((), jnp.int32)
    effective = lax.dynamic_update_slice(kv_cache, restored, (zero_index, zero_index, (failed_ctx * CTX_DEV).astype(jnp.int32), zero_index, zero_index))
    begins = (jnp.cumsum(new_lengths, axis=1) - new_lengths).astype(jnp.int32)
    ctx_ids = jnp.arange(N_CTX, dtype=jnp.int32)
    shard_rank = jnp.clip(ctx_ids - 1, 0, NEW_SHARDS - 1)
    begin_at = begins[:, shard_rank]
    length_at = new_lengths[:, shard_rank]
    slot_ids = jnp.arange(CAP, dtype=jnp.int32)
    usable = (slot_ids[None, None, :] < length_at[:, :, None]) & (ctx_ids != 0)[None, :, None]
    source_rows = jnp.where(usable, begin_at[:, :, None] + slot_ids[None, None, :], 0).reshape(SEQS, N_CTX * CAP).astype(jnp.int32)
    taken = jax.vmap(lambda cache_rows, row_ids: jnp.take(cache_rows, row_ids, axis=1), in_axes=(1, 0), out_axes=1)(effective, source_rows)
    new_cache = jnp.where(usable.reshape(SEQS, N_CTX * CAP)[None, :, :, None, None], taken, jnp.zeros((), taken.dtype))
    score_scale = 1.0 / math.sqrt(HD)
    step_ids = jnp.arange(STEPS, dtype=jnp.int32)
    causal = step_ids[None, :] <= step_ids[:, None]

    def attend_one(inputs):
        cache_keys, cache_values, query_rows, fresh_keys, fresh_values = inputs
        grouped = query_rows.reshape(STEPS, KVH, GROUP, HD).astype(jnp.float32)
        scores = jnp.einsum('tkgd,pkd->ktgp', grouped, cache_keys.astype(jnp.float32)) * score_scale
        fresh = jnp.einsum('tkgd,ukd->ktgu', grouped, fresh_keys.astype(jnp.float32)) * score_scale
        fresh = jnp.where(causal[None, :, None, :], fresh, -jnp.inf)
        highest = jnp.maximum(lax.optimization_barrier(jnp.max(scores, axis=-1)), lax.optimization_barrier(jnp.max(fresh, axis=-1)))
        weights = jnp.exp(scores - highest[..., None])
        fresh_weights = jnp.exp(fresh - highest[..., None])
        totals = lax.optimization_barrier(jnp.sum(weights, axis=-1)) + lax.optimization_barrier(jnp.sum(fresh_weights, axis=-1))
        rounded = lax.optimization_barrier(weights.astype(jnp.bfloat16)).astype(jnp.float32)
        fresh_rounded = lax.optimization_barrier(fresh_weights.astype(jnp.bfloat16)).astype(jnp.float32)
        mixture = jnp.einsum('ktgp,pkd->ktgd', rounded, cache_values.astype(jnp.float32))
        mixture = mixture + jnp.einsum('ktgu,ukd->ktgd', fresh_rounded, fresh_values.astype(jnp.float32))
        result = (mixture / totals[..., None]).transpose(1, 0, 2, 3).reshape(STEPS, QH, HD).astype(jnp.bfloat16)
        log_rows = (highest + jnp.log(totals)).transpose(1, 0, 2).reshape(STEPS, QH)
        return (result, log_rows)
    attended, log_total = lax.map(attend_one, (effective[0], effective[1], queries, new_kv[0], new_kv[1]))
    return (new_cache, attended, log_total)
```

```python
import functools
import math

import jax
import jax.numpy as jnp
from jax import lax
from jax.experimental import pallas as pl
from jax.experimental.pallas import tpu as pltpu
from jax.sharding import PartitionSpec as P

F32 = jnp.float32
BF16 = jnp.bfloat16
MESH = pl.DeviceIdType.MESH

far_below = -1e30

BLK = 128
N = 16
NB = 8
MP = 4
HD = 128
CTX = 1024
CAP = 1216
PIECE = CTX // N
ROWS = 2 * PIECE
PACK = ROWS + 16
PART = HD + 16

RS_LEFT, RS_RIGHT = 8, 7
AG_LEFT, AG_RIGHT = 8, 7
PART_LEFT, PART_RIGHT = 9, 6
A_PARTS = 16


def dot_tt(a, b):
    return lax.dot_general(a, b, (((1,), (1,)), ((), ())), preferred_element_type=F32)


def dot_sum_rows(a, b):
    return lax.dot_general(a, b, (((0,), (0,)), ((), ())), preferred_element_type=F32)


def iota(shape, dim):
    return lax.broadcasted_iota(jnp.int32, shape, dim)


def split_three(x):
    hi = x.astype(BF16).astype(F32)
    rest = x - hi
    mid = rest.astype(BF16).astype(F32)
    return hi, mid, rest - mid


def kernel(kv_hbm, codes_hbm, scales_hbm, shift_hbm, failed_hbm, lengths_hbm, q_hbm, fresh_hbm,
           out, att, logs,
           kv, codes, scales, shift, failed, lengths, q, fresh,
           lower, scale_tiles, lbuf, rbuf, xbuf, msgs, parts, qpad, score, own_mix, lost_mix, ext,
           in_sem, a_send, a_recv, l_send, l_recv, r_send, r_recv, x_send, x_recv,
           gl_send, gl_recv, gr_send, gr_recv, pl_send, pl_recv, pr_send, pr_recv):
    z = lax.axis_index("ctx")
    g = lax.axis_index("batch")
    k = lax.axis_index("mp")

    fetch = [
        pltpu.make_async_copy(source, target, in_sem.at[n])
        for n, (source, target) in enumerate((
            (codes_hbm, codes), (failed_hbm, failed), (shift_hbm, shift), (scales_hbm, scales),
            (kv_hbm, kv), (q_hbm, q), (fresh_hbm, fresh), (lengths_hbm, lengths)))
    ]
    for copy in fetch:
        copy.start()

    def ring(c):
        return lax.rem(c + 2 * N, N)

    up, down = ring(z + 1), ring(z - 1)
    g_to, g_from = lax.rem(g + NB - 1, NB), lax.rem(g + 1, NB)

    barrier = pltpu.get_barrier_semaphore()
    for c in (up, down):
        pl.semaphore_signal(barrier, inc=1, device_id=(c, g, k), device_id_type=MESH)
    for j in range(MP):
        pl.semaphore_signal(barrier, inc=1, device_id=(z, g_to, j), device_id_type=MESH)
        pl.semaphore_signal(barrier, inc=1, device_id=(z, g_from, j), device_id_type=MESH)

    for copy in fetch[:4]:
        copy.wait()
    fc = lax.rem(failed[0], N)
    lane = iota((16, HD), 1)
    row = iota((16, HD), 0)

    for p in range(2):
        both = scales[p].astype(F32)
        for b in range(CTX // BLK):
            tile = jnp.where(row == 0, both[0:1, b:b + 1], jnp.where(row == 1, both[1:2, b:b + 1], 0.0))
            scale_tiles[b, p] = tile.astype(BF16)

    def mine(d):
        return lax.rem(fc + shift[d // 2], N) == z

    def select(d, buf, t, p, first):
        start = pl.multiple_of(d * PIECE, PIECE)
        own = mine(d)
        for s in range(2):
            rows = slice(s * PIECE, (s + 1) * PIECE)
            here = codes[2 * p + s, pl.ds(start, PIECE), :]
            buf[t, p, rows, :] = here if first else jnp.where(own, here, buf[t, p, rows, :])
        here = scale_tiles[d // 2, p]
        buf[t, p, ROWS:, :] = here if first else jnp.where(own, here, buf[t, p, ROWS:, :])

    def rs_copy(buf, t, p, target, send, recv):
        return pltpu.make_async_remote_copy(
            src_ref=buf.at[t, p], dst_ref=buf.at[t + 1, p], send_sem=send.at[t, p], recv_sem=recv.at[t, p],
            device_id=(target, g, k), device_id_type=MESH)

    def l_copy(t, p):
        return rs_copy(lbuf, t, p, down, l_send, l_recv)

    def r_copy(t, p):
        return rs_copy(rbuf, t, p, up, r_send, r_recv)

    def ag_copy(t, p, target, source, send, recv):
        return pltpu.make_async_remote_copy(
            src_ref=msgs.at[source, p], dst_ref=msgs.at[source, p], send_sem=send.at[t, p], recv_sem=recv.at[t, p],
            device_id=(target, g, k), device_id_type=MESH)

    def gl_copy(t, p):
        return ag_copy(t, p, down, ring(z + t), gl_send, gl_recv)

    def gl_arrival(t, p):
        return ag_copy(t, p, down, ring(z + t + 1), gl_send, gl_recv)

    def gr_copy(t, p):
        return ag_copy(t, p, up, ring(z - t), gr_send, gr_recv)

    def gr_arrival(t, p):
        return ag_copy(t, p, up, ring(z - t - 1), gr_send, gr_recv)

    def part_copy(t, target, source, send, recv):
        return pltpu.make_async_remote_copy(
            src_ref=parts.at[source], dst_ref=parts.at[source], send_sem=send.at[t], recv_sem=recv.at[t],
            device_id=(target, g, k), device_id_type=MESH)

    def a_copy(n):
        rows = slice(n * (CTX // A_PARTS), (n + 1) * (CTX // A_PARTS))
        return pltpu.make_async_remote_copy(
            src_ref=kv.at[:, rows, :], dst_ref=lower.at[:, rows, :], send_sem=a_send.at[n], recv_sem=a_recv.at[n],
            device_id=(up, g, k), device_id_type=MESH)

    a_started = [0]

    def a_step(count=1):
        first = a_started[0]
        last = min(first + count, A_PARTS)
        a_started[0] = last

        @pl.when(z != N - 1)
        def _():
            for n in range(first, last):
                a_copy(n).start()

    part_step_at = [0]

    def part_step():
        t = part_step_at[0]
        part_step_at[0] = t + 1
        if t < PART_LEFT:
            if t > 0:
                part_copy(t - 1, down, ring(z + t), pl_send, pl_recv).wait_recv()
            part_copy(t, down, ring(z + t), pl_send, pl_recv).start()
        if t < PART_RIGHT:
            if t > 0:
                part_copy(t - 1, up, ring(z - t), pr_send, pr_recv).wait_recv()
            part_copy(t, up, ring(z - t), pr_send, pr_recv).start()

    for p in range(2):
        select(ring(z - RS_LEFT), lbuf, 0, p, True)
        select(ring(z + RS_RIGHT), rbuf, 0, p, True)
    pl.semaphore_wait(barrier, 2 + 2 * MP)
    for p in range(2):
        l_copy(0, p).start()
        r_copy(0, p).start()
    for copy in fetch[4:]:
        copy.wait()
    a_step()

    half = iota((HD, HD), 0) < HD // 2
    queries = q[...]
    zero = jnp.zeros((HD, HD), BF16)
    qpad[0] = jnp.where(half, queries, zero)
    qpad[1] = jnp.where(half, zero, queries)
    first_half = iota((1, HD), 1) < HD // 2
    scaling = 1.0 / math.sqrt(HD)
    alive = z != fc
    CH = 256

    def scores_of(k0, k1):
        return (dot_tt(k0, qpad[0]) + dot_tt(k1, qpad[1])) * scaling

    def weigh(s, top, v0, v1):
        w = jnp.exp(s - top)
        total = jnp.sum(w, axis=0, keepdims=True)
        w0 = jnp.where(first_half, w, 0.0).astype(BF16)
        w1 = jnp.where(first_half, 0.0, w).astype(BF16)
        return total, dot_sum_rows(v0, w0) + dot_sum_rows(v1, w1)

    own = {"top": jnp.full((1, HD), far_below, F32), "total": jnp.zeros((1, HD), F32)}

    def score_part(n):
        rows = slice(n * CH, (n + 1) * CH)
        s = scores_of(kv[0, rows, :], kv[1, rows, :])
        s = jnp.where(alive, s, far_below)
        score[rows, :] = s
        own["top"] = jnp.maximum(own["top"], jnp.max(s, axis=0, keepdims=True))

    def weigh_part(n):
        rows = slice(n * CH, (n + 1) * CH)
        total, mix = weigh(score[rows, :], own["top"], kv[2, rows, :], kv[3, rows, :])
        own["total"] = own["total"] + total
        own_mix[...] = mix if n == 0 else own_mix[...] + mix

    def own_done():
        parts[z, :HD, :] = jnp.where(alive, own_mix[...], 0.0).astype(BF16)
        tile = jnp.zeros((16, HD), F32)
        total = jnp.where(alive, own["total"], 0.0)
        for n, piece in enumerate(split_three(own["top"]) + split_three(total)):
            tile = jnp.where(row == n, piece, tile)
        parts[z, HD:, :] = tile.astype(BF16)
        part_step()

    fresh_part = {}

    def fresh_keys():
        fresh_rows = fresh[...]
        s = dot_tt(fresh_rows, queries) * scaling
        usable = (row < 8) & (row // 4 == lane // 64) & (lax.rem(row, 4) <= lax.rem(lane, 64) // 16)
        s = jnp.where(usable, s, far_below)
        top = jnp.max(s, axis=0, keepdims=True)
        w = jnp.where(usable, jnp.exp(s - top), 0.0)
        fresh_part["total"] = jnp.sum(w, axis=0, keepdims=True)
        fresh_part["top"] = top
        w = jnp.concatenate([jnp.zeros((8, HD), F32), w[:8]], axis=0).astype(BF16)
        fresh_part["mix"] = dot_sum_rows(fresh_rows, w)

    work = {0: [lambda n=n: score_part(n) for n in range(4)],
            1: [lambda n=n: weigh_part(n) for n in range(2)],
            2: [lambda n=n: weigh_part(n) for n in range(2, 4)] + [own_done],
            3: [part_step], 4: [part_step], 5: [part_step], 6: [part_step], 7: [part_step]}

    for thunk in work[0]:
        thunk()
    for t in range(1, max(RS_LEFT, RS_RIGHT)):
        for p in range(2):
            if t < RS_LEFT:
                l_copy(t - 1, p).wait_recv()
                select(ring(z - RS_LEFT + t), lbuf, t, p, False)
                l_copy(t, p).start()
            if t < RS_RIGHT:
                r_copy(t - 1, p).wait_recv()
                select(ring(z + RS_RIGHT - t), rbuf, t, p, False)
                r_copy(t, p).start()
        a_step()
        for thunk in work.get(t, []):
            thunk()

    def x_copy(j, p, slot):
        return pltpu.make_async_remote_copy(
            src_ref=lbuf.at[RS_LEFT, p], dst_ref=xbuf.at[p, slot],
            send_sem=x_send.at[j, p], recv_sem=x_recv.at[slot, p],
            device_id=(z, g_to, j), device_id_type=MESH)

    from_right = ring(lax.rem(fc + shift[z // 2], N) - z) <= RS_LEFT
    for p in range(2):
        r_copy(RS_RIGHT - 1, p).wait_recv()
        l_copy(RS_LEFT - 1, p).wait_recv()
        lbuf[RS_LEFT, p] = jnp.where(from_right, lbuf[RS_LEFT, p], rbuf[RS_RIGHT, p])
        select(z, lbuf, RS_LEFT, p, False)
        for j in range(MP):
            x_copy(j, p, k).start()
    a_step(2)
    part_step()
    fresh_keys()

    shared = iota((HD, HD), 0) & iota((HD, HD), 1)
    shared = shared ^ (shared >> 4)
    shared = shared ^ (shared >> 2)
    shared = (shared ^ (shared >> 1)) & 1
    signs = (1 - 2 * shared).astype(F32).astype(BF16)

    norm = 1.0 / math.sqrt(MP * HD)
    for p in range(2):
        mixed = [None] * 2
        for j in range(MP):
            x_copy(j, p, j).wait_recv()
            common = k & j
            odd = (common ^ (common >> 1)) & 1
            coef = jnp.where(odd == 1, -norm, norm).astype(F32)
            scale_rows = xbuf[p, j, ROWS:, :].astype(F32)
            turned = jnp.dot(xbuf[p, j, :ROWS, :], signs, preferred_element_type=F32)
            for s in range(2):
                term = turned[s * PIECE:(s + 1) * PIECE] * scale_rows[s:s + 1, :] * coef
                mixed[s] = term if j == 0 else mixed[s] + term
        for s in range(2):
            msgs[z, p, s * PIECE:(s + 1) * PIECE, :] = mixed[s].astype(BF16)
        gl_copy(0, p).start()
        gr_copy(0, p).start()

    lost = {}

    def lost_pieces(pieces):
        keys = [jnp.concatenate([msgs[c, 0, s * PIECE:(s + 1) * PIECE, :] for c in pieces], axis=0) for s in range(2)]
        values = [jnp.concatenate([msgs[c, 1, s * PIECE:(s + 1) * PIECE, :] for c in pieces], axis=0) for s in range(2)]
        s = scores_of(*keys)
        top = jnp.max(s, axis=0, keepdims=True)
        if lost:
            top = jnp.maximum(top, lost["top"])
        total, mix = weigh(s, top, *values)
        if lost:
            factor = jnp.exp(lost["top"] - top)
            total = total + lost["total"] * factor
            mix = mix + lost_mix[...] * factor
        lost_mix[...] = mix
        lost["top"], lost["total"] = top, total
        for c in pieces:
            rows = pl.ds(pl.multiple_of(c * PIECE, PIECE), PIECE)
            target = pl.ds(pl.multiple_of(CTX + c * PIECE, PIECE), PIECE)
            for i in range(4):
                rebuilt = msgs[c, i // 2, (i % 2) * PIECE:(i % 2 + 1) * PIECE, :]
                ext[i, target, :] = jnp.where(z == fc, rebuilt, kv[i, rows, :]).astype(F32)

    lost_pieces([z])
    a_step()
    part_step()
    steps = max(AG_LEFT, AG_RIGHT)
    for t in range(1, steps + 1):
        arrived = []
        for p in range(2):
            if t <= AG_LEFT:
                gl_arrival(t - 1, p).wait_recv()
                if t < AG_LEFT:
                    gl_copy(t, p).start()
            if t <= AG_RIGHT:
                gr_arrival(t - 1, p).wait_recv()
                if t < AG_RIGHT:
                    gr_copy(t, p).start()
        if t <= AG_LEFT:
            arrived.append(ring(z + t))
        if t <= AG_RIGHT:
            arrived.append(ring(z - t))
        a_step()
        part_step()
        lost_pieces(arrived)
    a_step(A_PARTS)
    while part_step_at[0] < max(PART_LEFT, PART_RIGHT):
        part_step()
    part_copy(PART_LEFT - 1, down, ring(z + PART_LEFT), pl_send, pl_recv).wait_recv()
    part_copy(PART_RIGHT - 1, up, ring(z - PART_RIGHT), pr_send, pr_recv).wait_recv()

    tops, totals = [fresh_part["top"], lost["top"]], [fresh_part["total"], lost["total"]]
    for c in range(N):
        tile = parts[c, HD:, :].astype(F32)
        tops.append(tile[0:1] + tile[1:2] + tile[2:3])
        totals.append(tile[3:4] + tile[4:5] + tile[5:6])
    top = functools.reduce(jnp.maximum, tops)
    factors = [jnp.exp(v - top) for v in tops]
    total = functools.reduce(jnp.add, [v * f for v, f in zip(totals, factors)])
    mix = fresh_part["mix"] * factors[0] + lost_mix[...] * factors[1]
    for c in range(N):
        mix = mix + parts[c, :HD, :].astype(F32) * factors[c + 2]
    att[...] = jnp.transpose(mix / total).astype(BF16)
    log_row = top + jnp.log(total)
    for n in range(8):
        turned = log_row if n == 0 else pltpu.roll(log_row, HD - 16 * n, 1)
        logs[n // 4, n % 4:n % 4 + 1, :] = turned[:, :16]

    @pl.when(z != 0)
    def _():
        for n in range(A_PARTS):
            a_copy(n).wait_recv()

    for c in range(N):
        rows = slice(c * PIECE, (c + 1) * PIECE)
        for i in range(4):
            rebuilt = msgs[c, i // 2, (i % 2) * PIECE:(i % 2 + 1) * PIECE, :]
            ext[i, rows, :] = jnp.where(z - 1 == fc, rebuilt, lower[i, rows, :]).astype(F32)
    for i in range(4):
        ext[i, 2 * CTX:, :] = jnp.zeros((CAP - CTX, HD), F32)
    for seq in range(2):
        begin = jnp.int32(0)
        length = jnp.int32(0)
        for j in range(N - 1):
            size = lengths[seq, j]
            begin = begin + jnp.where(j < z - 1, size, 0)
            length = jnp.where(j == z - 1, size, length)
        offset = jnp.clip(begin - (z - 1) * CTX, 0, CTX)
        slot = iota((PIECE, HD), 0)
        for p in range(2):
            for n in range(CAP // PIECE):
                rows = ext[2 * p + seq, pl.ds(offset + n * PIECE, PIECE), :]
                rows = jnp.where(slot + n * PIECE < length, rows, 0.0)
                out[2 * p + seq, n * PIECE:(n + 1) * PIECE, :] = rows.astype(BF16)

    for p in range(2):
        for t in range(RS_LEFT):
            l_copy(t, p).wait_send()
        for t in range(RS_RIGHT):
            r_copy(t, p).wait_send()
        for j in range(MP):
            x_copy(j, p, k).wait_send()
        for t in range(AG_LEFT):
            gl_copy(t, p).wait_send()
        for t in range(AG_RIGHT):
            gr_copy(t, p).wait_send()
    for t in range(PART_LEFT):
        part_copy(t, down, ring(z + t), pl_send, pl_recv).wait_send()
    for t in range(PART_RIGHT):
        part_copy(t, up, ring(z - t), pr_send, pr_recv).wait_send()

    @pl.when(z != N - 1)
    def _():
        for n in range(A_PARTS):
            a_copy(n).wait_send()


def body(kv_cache, backup_codes, backup_scales, block_shift, failed, new_lengths, queries, new_kv):
    vmem = pl.BlockSpec(memory_space=pltpu.VMEM)
    hbm = pl.BlockSpec(memory_space=pltpu.HBM)
    dma = pltpu.SemaphoreType.DMA
    out, att, logs = pl.pallas_call(
        kernel,
        out_shape=(
            jax.ShapeDtypeStruct((4, CAP, HD), BF16),
            jax.ShapeDtypeStruct((HD, HD), BF16),
            jax.ShapeDtypeStruct((2, 4, 16), F32),
        ),
        in_specs=[hbm] * 8,
        out_specs=(vmem, vmem, vmem),
        scratch_shapes=[
            pltpu.VMEM((4, CTX, HD), BF16),
            pltpu.VMEM((4, CTX, HD), BF16),
            pltpu.VMEM((2, 2, CTX // BLK), BF16),
            pltpu.SMEM((CTX // BLK,), jnp.int32),
            pltpu.SMEM((1,), jnp.int32),
            pltpu.SMEM((2, N - 1), jnp.int32),
            pltpu.VMEM((HD, HD), BF16),
            pltpu.VMEM((16, HD), BF16),
            pltpu.VMEM((4, CTX, HD), BF16),
            pltpu.VMEM((CTX // BLK, 2, 16, HD), BF16),
            pltpu.VMEM((RS_LEFT + 1, 2, PACK, HD), BF16),
            pltpu.VMEM((RS_RIGHT + 1, 2, PACK, HD), BF16),
            pltpu.VMEM((2, MP, PACK, HD), BF16),
            pltpu.VMEM((N, 2, ROWS, HD), BF16),
            pltpu.VMEM((N, PART, HD), BF16),
            pltpu.VMEM((2, HD, HD), BF16),
            pltpu.VMEM((CTX, HD), F32),
            pltpu.VMEM((HD, HD), F32),
            pltpu.VMEM((HD, HD), F32),
            pltpu.VMEM((4, CTX + CAP, HD), F32),
            dma((8,)),
            dma((A_PARTS,)), dma((A_PARTS,)),
            dma((RS_LEFT, 2)), dma((RS_LEFT, 2)),
            dma((RS_RIGHT, 2)), dma((RS_RIGHT, 2)),
            dma((MP, 2)), dma((MP, 2)),
            dma((AG_LEFT, 2)), dma((AG_LEFT, 2)),
            dma((AG_RIGHT, 2)), dma((AG_RIGHT, 2)),
            dma((PART_LEFT,)), dma((PART_LEFT,)),
            dma((PART_RIGHT,)), dma((PART_RIGHT,)),
        ],
        compiler_params=pltpu.CompilerParams(
            collective_id=0, has_side_effects=True, vmem_limit_bytes=56 * 1024 * 1024),
        cost_estimate=pl.CostEstimate(flops=10**8, bytes_accessed=4 * 10**6, transcendentals=2 * 10**5),
    )(
        kv_cache.reshape(4, CTX, HD),
        backup_codes.reshape(4, CTX, HD),
        backup_scales.reshape(2, 2, CTX // BLK),
        block_shift,
        failed,
        new_lengths,
        queries.reshape(HD, HD),
        new_kv.reshape(16, HD),
    )
    return (
        out.reshape(2, 2, CAP, 1, HD),
        att.reshape(queries.shape),
        logs,
    )


def solution(mesh):
    return jax.shard_map(
        body,
        mesh=mesh,
        in_specs=(
            P(None, "batch", "ctx", "mp", None),
            P(None, "batch", "ctx", "mp", None),
            P(None, "batch", "ctx", "mp"),
            P(),
            P(),
            P("batch", None),
            P("batch", None, "mp", None),
            P(None, "batch", None, "mp", None),
        ),
        out_specs=(
            P(None, "batch", "ctx", "mp", None),
            P("batch", None, "mp", None),
            P("batch", None, "mp"),
        ),
        check_vma=False,
    )
```

```python
import functools
import math

import jax
import jax.numpy as jnp
from jax import lax
from jax.experimental import pallas as pl
from jax.experimental.pallas import tpu as pltpu
from jax.sharding import PartitionSpec as P

F32 = jnp.float32
BF16 = jnp.bfloat16
MESH = pl.DeviceIdType.MESH

far_below = -1e30

BLK = 128
N = 16
NB = 8
MP = 4
HD = 128
CTX = 1024
CAP = 1216
PIECE = CTX // N
ROWS = 2 * PIECE
PACK = ROWS + 16
PART = HD + 16

RS_LEFT, RS_RIGHT = 10, 5
AG_LEFT, AG_RIGHT = 10, 5
PART_LEFT, PART_RIGHT = 15, 0
A_PARTS = 16


def dot_tt(a, b):
    return lax.dot_general(a, b, (((1,), (1,)), ((), ())), preferred_element_type=F32)


def dot_sum_rows(a, b):
    return lax.dot_general(a, b, (((0,), (0,)), ((), ())), preferred_element_type=F32)


def iota(shape, dim):
    return lax.broadcasted_iota(jnp.int32, shape, dim)


def split_three(x):
    hi = x.astype(BF16).astype(F32)
    rest = x - hi
    mid = rest.astype(BF16).astype(F32)
    return hi, mid, rest - mid


def kernel(kv_hbm, codes_hbm, scales_hbm, shift_hbm, failed_hbm, lengths_hbm, q_hbm, fresh_hbm,
           out, att, logs,
           kv, codes, scales, shift, failed, lengths, q, fresh,
           lower, scale_tiles, lbuf, rbuf, xbuf, msgs, parts, qpad, score, own_mix, lost_mix, ext,
           in_sem, a_send, a_recv, l_send, l_recv, r_send, r_recv, x_send, x_recv,
           gl_send, gl_recv, gr_send, gr_recv, pl_send, pl_recv, pr_send, pr_recv):
    z = lax.axis_index("ctx")
    g = lax.axis_index("batch")
    k = lax.axis_index("mp")

    fetch = [
        pltpu.make_async_copy(source, target, in_sem.at[n])
        for n, (source, target) in enumerate((
            (codes_hbm, codes), (failed_hbm, failed), (shift_hbm, shift), (scales_hbm, scales),
            (kv_hbm, kv), (q_hbm, q), (fresh_hbm, fresh), (lengths_hbm, lengths)))
    ]
    for copy in fetch:
        copy.start()

    def ring(c):
        return lax.rem(c + 2 * N, N)

    up, down = ring(z + 1), ring(z - 1)
    g_to, g_from = lax.rem(g + NB - 1, NB), lax.rem(g + 1, NB)

    barrier = pltpu.get_barrier_semaphore()
    for c in (up, down):
        pl.semaphore_signal(barrier, inc=1, device_id=(c, g, k), device_id_type=MESH)
    for j in range(MP):
        pl.semaphore_signal(barrier, inc=1, device_id=(z, g_to, j), device_id_type=MESH)
        pl.semaphore_signal(barrier, inc=1, device_id=(z, g_from, j), device_id_type=MESH)

    for copy in fetch[:4]:
        copy.wait()
    fc = lax.rem(failed[0], N)
    lane = iota((16, HD), 1)
    row = iota((16, HD), 0)

    for p in range(2):
        both = scales[p].astype(F32)
        for b in range(CTX // BLK):
            tile = jnp.where(row == 0, both[0:1, b:b + 1], jnp.where(row == 1, both[1:2, b:b + 1], 0.0))
            scale_tiles[b, p] = tile.astype(BF16)

    def mine(d):
        return lax.rem(fc + shift[d // 2], N) == z

    def select(d, buf, t, p, first):
        start = pl.multiple_of(d * PIECE, PIECE)
        own = mine(d)
        for s in range(2):
            rows = slice(s * PIECE, (s + 1) * PIECE)
            here = codes[2 * p + s, pl.ds(start, PIECE), :]
            buf[t, p, rows, :] = here if first else jnp.where(own, here, buf[t, p, rows, :])
        here = scale_tiles[d // 2, p]
        buf[t, p, ROWS:, :] = here if first else jnp.where(own, here, buf[t, p, ROWS:, :])

    def rs_copy(buf, t, p, target, send, recv):
        return pltpu.make_async_remote_copy(
            src_ref=buf.at[t, p], dst_ref=buf.at[t + 1, p], send_sem=send.at[t, p], recv_sem=recv.at[t, p],
            device_id=(target, g, k), device_id_type=MESH)

    def l_copy(t, p):
        return rs_copy(lbuf, t, p, down, l_send, l_recv)

    def r_copy(t, p):
        return rs_copy(rbuf, t, p, up, r_send, r_recv)

    def ag_copy(t, p, target, source, send, recv):
        return pltpu.make_async_remote_copy(
            src_ref=msgs.at[source, p], dst_ref=msgs.at[source, p], send_sem=send.at[t, p], recv_sem=recv.at[t, p],
            device_id=(target, g, k), device_id_type=MESH)

    def gl_copy(t, p):
        return ag_copy(t, p, down, ring(z + t), gl_send, gl_recv)

    def gl_arrival(t, p):
        return ag_copy(t, p, down, ring(z + t + 1), gl_send, gl_recv)

    def gr_copy(t, p):
        return ag_copy(t, p, up, ring(z - t), gr_send, gr_recv)

    def gr_arrival(t, p):
        return ag_copy(t, p, up, ring(z - t - 1), gr_send, gr_recv)

    def part_copy(t, target, source, send, recv):
        return pltpu.make_async_remote_copy(
            src_ref=parts.at[source], dst_ref=parts.at[source], send_sem=send.at[t], recv_sem=recv.at[t],
            device_id=(target, g, k), device_id_type=MESH)

    def a_copy(n):
        rows = slice(n * (CTX // A_PARTS), (n + 1) * (CTX // A_PARTS))
        return pltpu.make_async_remote_copy(
            src_ref=kv.at[:, rows, :], dst_ref=lower.at[:, rows, :], send_sem=a_send.at[n], recv_sem=a_recv.at[n],
            device_id=(up, g, k), device_id_type=MESH)

    a_started = [0]

    def a_step(count=1):
        first = a_started[0]
        last = min(first + count, A_PARTS)
        a_started[0] = last

        @pl.when(z != N - 1)
        def _():
            for n in range(first, last):
                a_copy(n).start()

    part_step_at = [0]

    def part_step():
        t = part_step_at[0]
        part_step_at[0] = t + 1
        if t < PART_LEFT:
            if t > 0:
                part_copy(t - 1, down, ring(z + t), pl_send, pl_recv).wait_recv()
            part_copy(t, down, ring(z + t), pl_send, pl_recv).start()
        if t < PART_RIGHT:
            if t > 0:
                part_copy(t - 1, up, ring(z - t), pr_send, pr_recv).wait_recv()
            part_copy(t, up, ring(z - t), pr_send, pr_recv).start()

    for p in range(2):
        select(ring(z - RS_LEFT), lbuf, 0, p, True)
        select(ring(z + RS_RIGHT), rbuf, 0, p, True)
    pl.semaphore_wait(barrier, 2 + 2 * MP)
    for p in range(2):
        l_copy(0, p).start()
        r_copy(0, p).start()
    for copy in fetch[4:]:
        copy.wait()
    a_step()

    half = iota((HD, HD), 0) < HD // 2
    queries = q[...]
    zero = jnp.zeros((HD, HD), BF16)
    qpad[0] = jnp.where(half, queries, zero)
    qpad[1] = jnp.where(half, zero, queries)
    first_half = iota((1, HD), 1) < HD // 2
    scaling = 1.0 / math.sqrt(HD)
    alive = z != fc
    CH = 256

    def scores_of(k0, k1):
        return (dot_tt(k0, qpad[0]) + dot_tt(k1, qpad[1])) * scaling

    def weigh(s, top, v0, v1):
        w = jnp.exp(s - top)
        total = jnp.sum(w, axis=0, keepdims=True)
        w0 = jnp.where(first_half, w, 0.0).astype(BF16)
        w1 = jnp.where(first_half, 0.0, w).astype(BF16)
        return total, dot_sum_rows(v0, w0) + dot_sum_rows(v1, w1)

    own = {"top": jnp.full((1, HD), far_below, F32), "total": jnp.zeros((1, HD), F32)}

    def score_part(n):
        rows = slice(n * CH, (n + 1) * CH)
        s = scores_of(kv[0, rows, :], kv[1, rows, :])
        s = jnp.where(alive, s, far_below)
        score[rows, :] = s
        own["top"] = jnp.maximum(own["top"], jnp.max(s, axis=0, keepdims=True))

    def weigh_part(n):
        rows = slice(n * CH, (n + 1) * CH)
        total, mix = weigh(score[rows, :], own["top"], kv[2, rows, :], kv[3, rows, :])
        own["total"] = own["total"] + total
        own_mix[...] = mix if n == 0 else own_mix[...] + mix

    def own_done():
        parts[z, :HD, :] = jnp.where(alive, own_mix[...], 0.0).astype(BF16)
        tile = jnp.zeros((16, HD), F32)
        total = jnp.where(alive, own["total"], 0.0)
        for n, piece in enumerate(split_three(own["top"]) + split_three(total)):
            tile = jnp.where(row == n, piece, tile)
        parts[z, HD:, :] = tile.astype(BF16)
        part_step()

    fresh_part = {}

    def fresh_keys():
        fresh_rows = fresh[...]
        s = dot_tt(fresh_rows, queries) * scaling
        usable = (row < 8) & (row // 4 == lane // 64) & (lax.rem(row, 4) <= lax.rem(lane, 64) // 16)
        s = jnp.where(usable, s, far_below)
        top = jnp.max(s, axis=0, keepdims=True)
        w = jnp.where(usable, jnp.exp(s - top), 0.0)
        fresh_part["total"] = jnp.sum(w, axis=0, keepdims=True)
        fresh_part["top"] = top
        w = jnp.concatenate([jnp.zeros((8, HD), F32), w[:8]], axis=0).astype(BF16)
        fresh_part["mix"] = dot_sum_rows(fresh_rows, w)

    work = {0: [lambda n=n: score_part(n) for n in range(4)],
            1: [lambda n=n: weigh_part(n) for n in range(2)],
            2: [lambda n=n: weigh_part(n) for n in range(2, 4)] + [own_done],
            **{t: [part_step] for t in range(3, RS_LEFT)}}

    for thunk in work[0]:
        thunk()
    for t in range(1, max(RS_LEFT, RS_RIGHT)):
        for p in range(2):
            if t < RS_LEFT:
                l_copy(t - 1, p).wait_recv()
                select(ring(z - RS_LEFT + t), lbuf, t, p, False)
                l_copy(t, p).start()
            if t % 2 == 0 and t // 2 < RS_RIGHT:
                r_copy(t // 2 - 1, p).wait_recv()
                select(ring(z + RS_RIGHT - t // 2), rbuf, t // 2, p, False)
                r_copy(t // 2, p).start()
        a_step()
        for thunk in work.get(t, []):
            thunk()

    def x_copy(j, p, slot):
        return pltpu.make_async_remote_copy(
            src_ref=lbuf.at[RS_LEFT, p], dst_ref=xbuf.at[p, slot],
            send_sem=x_send.at[j, p], recv_sem=x_recv.at[slot, p],
            device_id=(z, g_to, j), device_id_type=MESH)

    from_right = ring(lax.rem(fc + shift[z // 2], N) - z) <= RS_LEFT
    for p in range(2):
        r_copy(RS_RIGHT - 1, p).wait_recv()
        l_copy(RS_LEFT - 1, p).wait_recv()
        lbuf[RS_LEFT, p] = jnp.where(from_right, lbuf[RS_LEFT, p], rbuf[RS_RIGHT, p])
        select(z, lbuf, RS_LEFT, p, False)
        for j in range(MP):
            x_copy(j, p, k).start()
    a_step(2)
    part_step()
    fresh_keys()

    shared = iota((HD, HD), 0) & iota((HD, HD), 1)
    shared = shared ^ (shared >> 4)
    shared = shared ^ (shared >> 2)
    shared = (shared ^ (shared >> 1)) & 1
    signs = (1 - 2 * shared).astype(F32).astype(BF16)

    norm = 1.0 / math.sqrt(MP * HD)
    for p in range(2):
        mixed = [None] * 2
        for j in range(MP):
            x_copy(j, p, j).wait_recv()
            common = k & j
            odd = (common ^ (common >> 1)) & 1
            coef = jnp.where(odd == 1, -norm, norm).astype(F32)
            scale_rows = xbuf[p, j, ROWS:, :].astype(F32)
            turned = jnp.dot(xbuf[p, j, :ROWS, :], signs, preferred_element_type=F32)
            for s in range(2):
                term = turned[s * PIECE:(s + 1) * PIECE] * scale_rows[s:s + 1, :] * coef
                mixed[s] = term if j == 0 else mixed[s] + term
        for s in range(2):
            msgs[z, p, s * PIECE:(s + 1) * PIECE, :] = mixed[s].astype(BF16)
        gl_copy(0, p).start()
        gr_copy(0, p).start()

    lost = {}

    def lost_pieces(pieces):
        keys = [jnp.concatenate([msgs[c, 0, s * PIECE:(s + 1) * PIECE, :] for c in pieces], axis=0) for s in range(2)]
        values = [jnp.concatenate([msgs[c, 1, s * PIECE:(s + 1) * PIECE, :] for c in pieces], axis=0) for s in range(2)]
        s = scores_of(*keys)
        top = jnp.max(s, axis=0, keepdims=True)
        if lost:
            top = jnp.maximum(top, lost["top"])
        total, mix = weigh(s, top, *values)
        if lost:
            factor = jnp.exp(lost["top"] - top)
            total = total + lost["total"] * factor
            mix = mix + lost_mix[...] * factor
        lost_mix[...] = mix
        lost["top"], lost["total"] = top, total
        for c in pieces:
            rows = pl.ds(pl.multiple_of(c * PIECE, PIECE), PIECE)
            target = pl.ds(pl.multiple_of(CTX + c * PIECE, PIECE), PIECE)
            for i in range(4):
                rebuilt = msgs[c, i // 2, (i % 2) * PIECE:(i % 2 + 1) * PIECE, :]
                ext[i, target, :] = jnp.where(z == fc, rebuilt, kv[i, rows, :]).astype(F32)

    lost_pieces([z])
    a_step()
    part_step()
    steps = max(AG_LEFT, AG_RIGHT)
    for t in range(1, steps + 1):
        arrived = []
        for p in range(2):
            if t <= AG_LEFT:
                gl_arrival(t - 1, p).wait_recv()
                if t < AG_LEFT:
                    gl_copy(t, p).start()
            if t % 2 == 0 and t // 2 <= AG_RIGHT:
                gr_arrival(t // 2 - 1, p).wait_recv()
                if t // 2 < AG_RIGHT:
                    gr_copy(t // 2, p).start()
        if t <= AG_LEFT:
            arrived.append(ring(z + t))
        if t % 2 == 0 and t // 2 <= AG_RIGHT:
            arrived.append(ring(z - t // 2))
        a_step()
        part_step()
        lost_pieces(arrived)
    a_step(A_PARTS)
    while part_step_at[0] < max(PART_LEFT, PART_RIGHT):
        part_step()
    part_copy(PART_LEFT - 1, down, ring(z + PART_LEFT), pl_send, pl_recv).wait_recv()

    tops, totals = [fresh_part["top"], lost["top"]], [fresh_part["total"], lost["total"]]
    for c in range(N):
        tile = parts[c, HD:, :].astype(F32)
        tops.append(tile[0:1] + tile[1:2] + tile[2:3])
        totals.append(tile[3:4] + tile[4:5] + tile[5:6])
    top = functools.reduce(jnp.maximum, tops)
    factors = [jnp.exp(v - top) for v in tops]
    total = functools.reduce(jnp.add, [v * f for v, f in zip(totals, factors)])
    mix = fresh_part["mix"] * factors[0] + lost_mix[...] * factors[1]
    for c in range(N):
        mix = mix + parts[c, :HD, :].astype(F32) * factors[c + 2]
    att[...] = jnp.transpose(mix / total).astype(BF16)
    log_row = top + jnp.log(total)
    for n in range(8):
        turned = log_row if n == 0 else pltpu.roll(log_row, HD - 16 * n, 1)
        logs[n // 4, n % 4:n % 4 + 1, :] = turned[:, :16]

    @pl.when(z != 0)
    def _():
        for n in range(A_PARTS):
            a_copy(n).wait_recv()

    for c in range(N):
        rows = slice(c * PIECE, (c + 1) * PIECE)
        for i in range(4):
            rebuilt = msgs[c, i // 2, (i % 2) * PIECE:(i % 2 + 1) * PIECE, :]
            ext[i, rows, :] = jnp.where(z - 1 == fc, rebuilt, lower[i, rows, :]).astype(F32)
    for i in range(4):
        ext[i, 2 * CTX:, :] = jnp.zeros((CAP - CTX, HD), F32)
    for seq in range(2):
        begin = jnp.int32(0)
        length = jnp.int32(0)
        for j in range(N - 1):
            size = lengths[seq, j]
            begin = begin + jnp.where(j < z - 1, size, 0)
            length = jnp.where(j == z - 1, size, length)
        offset = jnp.clip(begin - (z - 1) * CTX, 0, CTX)
        slot = iota((PIECE, HD), 0)
        for p in range(2):
            for n in range(CAP // PIECE):
                rows = ext[2 * p + seq, pl.ds(offset + n * PIECE, PIECE), :]
                rows = jnp.where(slot + n * PIECE < length, rows, 0.0)
                out[2 * p + seq, n * PIECE:(n + 1) * PIECE, :] = rows.astype(BF16)

    for p in range(2):
        for t in range(RS_LEFT):
            l_copy(t, p).wait_send()
        for t in range(RS_RIGHT):
            r_copy(t, p).wait_send()
        for j in range(MP):
            x_copy(j, p, k).wait_send()
        for t in range(AG_LEFT):
            gl_copy(t, p).wait_send()
        for t in range(AG_RIGHT):
            gr_copy(t, p).wait_send()
    for t in range(PART_LEFT):
        part_copy(t, down, ring(z + t), pl_send, pl_recv).wait_send()
    for t in range(PART_RIGHT):
        part_copy(t, up, ring(z - t), pr_send, pr_recv).wait_send()

    @pl.when(z != N - 1)
    def _():
        for n in range(A_PARTS):
            a_copy(n).wait_send()


def hand_over(source, att_source, log_source, out, att, logs, sems):
    pairs = [(source.at[i], out.at[i]) for i in range(4)] + [(att_source, att), (log_source, logs)]
    copies = [pltpu.make_async_copy(a, b, sems.at[n]) for n, (a, b) in enumerate(pairs)]
    for copy in copies:
        copy.start()
    for copy in copies:
        copy.wait()


def body(kv_cache, backup_codes, backup_scales, block_shift, failed, new_lengths, queries, new_kv):
    vmem = pl.BlockSpec(memory_space=pltpu.VMEM)
    hbm = pl.BlockSpec(memory_space=pltpu.HBM)
    dma = pltpu.SemaphoreType.DMA
    out, att, logs = pl.pallas_call(
        kernel,
        out_shape=(
            jax.ShapeDtypeStruct((4, CAP, HD), BF16),
            jax.ShapeDtypeStruct((HD, HD), BF16),
            jax.ShapeDtypeStruct((2, 4, 16), F32),
        ),
        in_specs=[hbm] * 8,
        out_specs=(vmem, vmem, vmem),
        scratch_shapes=[
            pltpu.VMEM((4, CTX, HD), BF16),
            pltpu.VMEM((4, CTX, HD), BF16),
            pltpu.VMEM((2, 2, CTX // BLK), BF16),
            pltpu.SMEM((CTX // BLK,), jnp.int32),
            pltpu.SMEM((1,), jnp.int32),
            pltpu.SMEM((2, N - 1), jnp.int32),
            pltpu.VMEM((HD, HD), BF16),
            pltpu.VMEM((16, HD), BF16),
            pltpu.VMEM((4, CTX, HD), BF16),
            pltpu.VMEM((CTX // BLK, 2, 16, HD), BF16),
            pltpu.VMEM((RS_LEFT + 1, 2, PACK, HD), BF16),
            pltpu.VMEM((RS_RIGHT + 1, 2, PACK, HD), BF16),
            pltpu.VMEM((2, MP, PACK, HD), BF16),
            pltpu.VMEM((N, 2, ROWS, HD), BF16),
            pltpu.VMEM((N, PART, HD), BF16),
            pltpu.VMEM((2, HD, HD), BF16),
            pltpu.VMEM((CTX, HD), F32),
            pltpu.VMEM((HD, HD), F32),
            pltpu.VMEM((HD, HD), F32),
            pltpu.VMEM((4, CTX + CAP, HD), F32),
            dma((8,)),
            dma((A_PARTS,)), dma((A_PARTS,)),
            dma((RS_LEFT, 2)), dma((RS_LEFT, 2)),
            dma((RS_RIGHT, 2)), dma((RS_RIGHT, 2)),
            dma((MP, 2)), dma((MP, 2)),
            dma((AG_LEFT, 2)), dma((AG_LEFT, 2)),
            dma((AG_RIGHT, 2)), dma((AG_RIGHT, 2)),
            dma((PART_LEFT,)), dma((PART_LEFT,)),
            dma((1,)), dma((1,)),
        ],
        compiler_params=pltpu.CompilerParams(
            collective_id=0, has_side_effects=True, vmem_limit_bytes=56 * 1024 * 1024),
        cost_estimate=pl.CostEstimate(flops=10**8, bytes_accessed=4 * 10**6, transcendentals=2 * 10**5),
    )(
        kv_cache.reshape(4, CTX, HD),
        backup_codes.reshape(4, CTX, HD),
        backup_scales.reshape(2, 2, CTX // BLK),
        block_shift,
        failed,
        new_lengths,
        queries.reshape(HD, HD),
        new_kv.reshape(16, HD),
    )
    out, att, logs = pl.pallas_call(
        hand_over,
        out_shape=(
            jax.ShapeDtypeStruct((4, CAP, HD), BF16),
            jax.ShapeDtypeStruct((HD, HD), BF16),
            jax.ShapeDtypeStruct((2, 4, 16), F32),
        ),
        in_specs=[hbm] * 3,
        out_specs=(hbm,) * 3,
        scratch_shapes=[dma((6,))],
        cost_estimate=pl.CostEstimate(flops=0, bytes_accessed=25 * 10**5, transcendentals=0),
    )(out, att, logs)
    return (
        out.reshape(2, 2, CAP, 1, HD),
        att.reshape(queries.shape),
        logs,
    )


def solution(mesh):
    return jax.shard_map(
        body,
        mesh=mesh,
        in_specs=(
            P(None, "batch", "ctx", "mp", None),
            P(None, "batch", "ctx", "mp", None),
            P(None, "batch", "ctx", "mp"),
            P(),
            P(),
            P("batch", None),
            P("batch", None, "mp", None),
            P(None, "batch", None, "mp", None),
        ),
        out_specs=(
            P(None, "batch", "ctx", "mp", None),
            P("batch", None, "mp", None),
            P("batch", None, "mp"),
        ),
        check_vma=False,
    )
```

```python
import functools
import math

import jax
import jax.numpy as jnp
from jax import lax
from jax.experimental import pallas as pl
from jax.experimental.pallas import tpu as pltpu
from jax.sharding import PartitionSpec as P

F32 = jnp.float32
BF16 = jnp.bfloat16
MESH = pl.DeviceIdType.MESH

far_below = -1e30

BLK = 128
N = 16
NB = 8
MP = 4
HD = 128
CTX = 1024
CAP = 1216
PIECE = CTX // N
ROWS = 2 * PIECE
PACK = ROWS + 16
BLOCKS = CTX // BLK
SUB = 8

HOPS = 5
A_PARTS = 16


def dot_tt(a, b):
    return lax.dot_general(a, b, (((1,), (1,)), ((), ())), preferred_element_type=F32)


def dot_sum_rows(a, b):
    return lax.dot_general(a, b, (((0,), (0,)), ((), ())), preferred_element_type=F32)


def iota(shape, dim):
    return lax.broadcasted_iota(jnp.int32, shape, dim)


def kernel(slots, kv_hbm, codes_hbm, scales_hbm, shift_hbm, failed_hbm, lengths_hbm, q_hbm, fresh_hbm,
           out, att, logs,
           kv, codes, scales, shift, failed, lengths, q, fresh,
           lower, bsend, bbuf, srow, xsend, xbuf, msgs, score, own_mix, stats, slices, merged, lost_mix, ext,
           in_sem, a_send, a_recv, b_send, b_recv, s_send, s_recv, x_send, x_recv,
           one_send, one_recv, two_send, two_recv, up_send, up_recv,
           st_send, st_recv, sl_send, sl_recv, me_send, me_recv):
    z = lax.axis_index("ctx")
    g = lax.axis_index("batch")
    k = lax.axis_index("mp")

    fetch = [
        pltpu.make_async_copy(source, target, in_sem.at[n])
        for n, (source, target) in enumerate((
            (codes_hbm, codes), (failed_hbm, failed), (shift_hbm, shift), (scales_hbm, scales),
            (kv_hbm, kv), (q_hbm, q), (fresh_hbm, fresh), (lengths_hbm, lengths)))
    ]
    for copy in fetch:
        copy.start()

    def ring(c):
        return lax.rem(c + 2 * N, N)

    g_to, g_from = lax.rem(g + NB - 1, NB), lax.rem(g + 1, NB)

    barrier = pltpu.get_barrier_semaphore()
    for o in range(1, N):
        pl.semaphore_signal(barrier, inc=1, device_id=(ring(z + o), g, k), device_id_type=MESH)
    for j in range(MP):
        pl.semaphore_signal(barrier, inc=1, device_id=(z, g_to, j), device_id_type=MESH)
        pl.semaphore_signal(barrier, inc=1, device_id=(z, g_from, j), device_id_type=MESH)

    for copy in fetch[:4]:
        copy.wait()
    fc = lax.rem(failed[0], N)
    lane = iota((16, HD), 1)
    row = iota((16, HD), 0)

    shifts = [shift[b] for b in range(BLOCKS)]
    holder = [lax.rem(fc + v, N) for v in shifts]
    rank = []
    for b in range(BLOCKS):
        before = jnp.int32(0)
        for e in range(b):
            before = before + jnp.where(shifts[e] == shifts[b], 1, 0)
        rank.append(jnp.minimum(before, slots - 1))
    def chosen(b, h, j):
        return (holder[b] == h) & (rank[b] == j)

    for j in range(slots):
        for p in range(2):
            pair = []
            for s in range(2):
                block = codes[2 * p + s, j * BLK:(j + 1) * BLK, :]
                for b in range(j + 1, BLOCKS):
                    block = jnp.where(chosen(b, z, j), codes[2 * p + s, b * BLK:(b + 1) * BLK, :], block)
                pair.append(block.astype(F32))
            for c in range(N):
                part = slice(c * SUB, (c + 1) * SUB)
                bsend[c, j, p] = jnp.concatenate([pair[0][part], pair[1][part]], axis=0).astype(BF16)
    line = jnp.zeros((1, HD), F32)
    for p in range(2):
        both = scales[p].astype(F32)
        for s in range(2):
            wide = jnp.concatenate([both[s:s + 1], jnp.zeros((1, HD - BLOCKS), F32)], axis=1)
            at = (2 * p + s) * BLOCKS
            line = line + (pltpu.roll(wide, at, 1) if at else wide)
    srow[z] = line
    bbuf[z] = bsend[z]

    def peer_copy(o, source, target, send, recv):
        return pltpu.make_async_remote_copy(
            src_ref=source, dst_ref=target, send_sem=send.at[o], recv_sem=recv.at[o],
            device_id=(ring(z + o), g, k), device_id_type=MESH)

    def b_copy(o):
        return peer_copy(o, bsend.at[ring(z + o)], bbuf.at[z], b_send, b_recv)

    def s_copy(o):
        return peer_copy(o, srow.at[z], srow.at[z], s_send, s_recv)

    def st_copy(o):
        return peer_copy(o, stats.at[z], stats.at[z], st_send, st_recv)

    def sl_copy(o):
        rows = pl.ds(pl.multiple_of(ring(z + o) * SUB, SUB), SUB)
        return peer_copy(o, own_mix.at[rows, :], slices.at[z], sl_send, sl_recv)

    def me_copy(o):
        return peer_copy(o, merged.at[z], merged.at[z], me_send, me_recv)

    order = [8, 7, 9, 6, 10, 5, 11, 4, 12, 3, 13, 2, 14, 1, 15]
    pl.semaphore_wait(barrier, N - 1 + 2 * MP)
    for o in order:
        b_copy(o).start()
        s_copy(o).start()

    def a_copy(n):
        rows = slice(n * (CTX // A_PARTS), (n + 1) * (CTX // A_PARTS))
        return pltpu.make_async_remote_copy(
            src_ref=kv.at[:, rows, :], dst_ref=lower.at[:, rows, :], send_sem=a_send.at[n], recv_sem=a_recv.at[n],
            device_id=(ring(z + 1), g, k), device_id_type=MESH)

    a_started = [0]

    def a_step(count):
        first = a_started[0]
        last = min(first + count, A_PARTS)
        a_started[0] = last

        @pl.when(z != N - 1)
        def _():
            for n in range(first, last):
                a_copy(n).start()

    for copy in fetch[4:]:
        copy.wait()

    half = iota((HD, HD), 0) < HD // 2
    queries = q[...]
    zero = jnp.zeros((HD, HD), BF16)
    q0, q1 = jnp.where(half, queries, zero), jnp.where(half, zero, queries)
    first_half = iota((1, HD), 1) < HD // 2
    scaling = 1.0 / math.sqrt(HD)
    alive = z != fc
    CH = 256

    top_own = jnp.full((1, HD), far_below, F32)
    for n in range(CTX // CH):
        rows = slice(n * CH, (n + 1) * CH)
        s = (dot_tt(kv[0, rows, :], q0) + dot_tt(kv[1, rows, :], q1)) * scaling
        s = jnp.where(alive, s, far_below)
        score[rows, :] = s
        top_own = jnp.maximum(top_own, jnp.max(s, axis=0, keepdims=True))
    total_own = jnp.zeros((1, HD), F32)
    for n in range(CTX // CH):
        rows = slice(n * CH, (n + 1) * CH)
        w = jnp.where(alive, jnp.exp(score[rows, :] - top_own), 0.0)
        total_own = total_own + jnp.sum(w, axis=0, keepdims=True)
        w0 = jnp.where(first_half, w, 0.0).astype(BF16)
        w1 = jnp.where(first_half, 0.0, w).astype(BF16)
        mix = dot_sum_rows(kv[2, rows, :], w0) + dot_sum_rows(kv[3, rows, :], w1)
        own_mix[...] = mix if n == 0 else own_mix[...] + mix
    stats[z, 0] = top_own
    stats[z, 1] = total_own
    slices[z] = own_mix[pl.ds(pl.multiple_of(z * SUB, SUB), SUB), :]

    fresh_rows = fresh[...]
    s = dot_tt(fresh_rows, queries) * scaling
    usable = (row < 8) & (row // 4 == lane // 64) & (lax.rem(row, 4) <= lax.rem(lane, 64) // 16)
    s = jnp.where(usable, s, far_below)
    top_fresh = jnp.max(s, axis=0, keepdims=True)
    w = jnp.where(usable, jnp.exp(s - top_fresh), 0.0)
    total_fresh = jnp.sum(w, axis=0, keepdims=True)
    w = jnp.concatenate([jnp.zeros((8, HD), F32), w[:8]], axis=0).astype(BF16)
    mix_fresh = dot_sum_rows(fresh_rows, w)

    shared = iota((HD, HD), 0) & iota((HD, HD), 1)
    shared = shared ^ (shared >> 4)
    shared = shared ^ (shared >> 2)
    shared = (shared ^ (shared >> 1)) & 1
    signs = (1 - 2 * shared).astype(F32).astype(BF16)

    for i in range(4):
        for n in range(CTX // CH):
            ext[i, CTX + n * CH:CTX + (n + 1) * CH, :] = kv[i, n * CH:(n + 1) * CH, :].astype(F32)
        ext[i, 2 * CTX:, :] = jnp.zeros((CAP - CTX, HD), F32)

    for o in order:
        b_copy(o).wait_recv()
        s_copy(o).wait_recv()
    tiles = [jnp.zeros((16, HD), F32) for _ in range(2)]
    for b in range(BLOCKS):
        line = srow[0]
        for h in range(1, N):
            line = jnp.where(holder[b] == h, srow[h], line)
        for p in range(2):
            for s in range(2):
                at = (2 * p + s) * BLOCKS + b
                tiles[p] = jnp.where(row == 2 * b + s, line[:, at:at + 1], tiles[p])

    def x_copy(j, p, slot):
        return pltpu.make_async_remote_copy(
            src_ref=xsend.at[p], dst_ref=xbuf.at[p, slot],
            send_sem=x_send.at[j, p], recv_sem=x_recv.at[slot, p],
            device_id=(z, g_to, j), device_id_type=MESH)

    for p in range(2):
        for b in range(BLOCKS):
            tile = bbuf[0, 0, p]
            for h in range(N):
                for j in range(min(slots, b + 1)):
                    if h + j > 0:
                        tile = jnp.where(chosen(b, h, j), bbuf[h, j, p], tile)
            xsend[p, b * 16:(b + 1) * 16, :] = tile
        xsend[p, ROWS:, :] = tiles[p].astype(BF16)
        for j in range(MP):
            x_copy(j, p, k).start()
    for o in order:
        st_copy(o).start()
        sl_copy(o).start()
    a_step(5)

    def one_copy(t, p, piece):
        return pltpu.make_async_remote_copy(
            src_ref=msgs.at[piece, p], dst_ref=msgs.at[piece, p], send_sem=one_send.at[t, p], recv_sem=one_recv.at[t, p],
            device_id=(ring(z - 1), g, k), device_id_type=MESH)

    def two_copy(t, p, piece):
        return pltpu.make_async_remote_copy(
            src_ref=msgs.at[piece, p], dst_ref=msgs.at[piece, p], send_sem=two_send.at[t, p], recv_sem=two_recv.at[t, p],
            device_id=(ring(z - 2), g, k), device_id_type=MESH)

    def up_copy(t, p, piece):
        return pltpu.make_async_remote_copy(
            src_ref=msgs.at[piece, p], dst_ref=msgs.at[piece, p], send_sem=up_send.at[t, p], recv_sem=up_recv.at[t, p],
            device_id=(ring(z + 1), g, k), device_id_type=MESH)

    norm = 1.0 / math.sqrt(MP * HD)
    for p in range(2):
        mixed = None
        for j in range(MP):
            x_copy(j, p, j).wait_recv()
            common = k & j
            odd = (common ^ (common >> 1)) & 1
            coef = jnp.where(odd == 1, -norm, norm).astype(F32)
            tile = xbuf[p, j, ROWS:, :].astype(F32)
            wide = jnp.concatenate([jnp.broadcast_to(tile[r:r + 1], (SUB, HD)) for r in range(16)], axis=0)
            term = jnp.dot(xbuf[p, j, :ROWS, :], signs, preferred_element_type=F32) * wide * coef
            mixed = term if j == 0 else mixed + term
        msgs[z, p] = mixed.astype(BF16)
        two_copy(0, p, z).start()
        up_copy(0, p, z).start()
        one_copy(0, p, z).start()

    lost = {}

    def lost_pieces(pieces):
        count = len(pieces)
        keys = jnp.concatenate([msgs[c, 0] for c in pieces], axis=0)
        values = jnp.concatenate([msgs[c, 1] for c in pieces], axis=0)
        matching = ((iota((ROWS * count, HD), 0) // SUB) & 1) == iota((ROWS * count, HD), 1) // (HD // 2)
        s = jnp.where(matching, dot_tt(keys, queries) * scaling, far_below)
        top = jnp.max(s, axis=0, keepdims=True)
        if lost:
            top = jnp.maximum(top, lost["top"])
        w = jnp.where(matching, jnp.exp(s - top), 0.0)
        total = jnp.sum(w, axis=0, keepdims=True)
        mix = dot_sum_rows(values, w.astype(BF16))
        if lost:
            factor = jnp.exp(lost["top"] - top)
            total = total + lost["total"] * factor
            mix = mix + lost_mix[...] * factor
        lost_mix[...] = mix
        lost["top"], lost["total"] = top, total
        for c in pieces:
            for p in range(2):
                for b in range(BLOCKS):
                    tile = msgs[c, p, b * 16:(b + 1) * 16, :].astype(F32)
                    rows = pl.ds(pl.multiple_of(CTX + b * BLK + c * SUB, SUB), SUB)
                    for s in range(2):
                        ext[2 * p + s, rows, :] = jnp.where(
                            z == fc, tile[s * SUB:(s + 1) * SUB], ext[2 * p + s, rows, :])

    a_step(2)
    lost_pieces([z])

    for o in order:
        st_copy(o).wait_recv()
        sl_copy(o).wait_recv()
    tops = [stats[c, 0] for c in range(N)]
    top_alive = functools.reduce(jnp.maximum, tops)
    factors = [jnp.exp(v - top_alive) for v in tops]
    total_alive = functools.reduce(jnp.add, [stats[c, 1] * factors[c] for c in range(N)])
    merged[z] = functools.reduce(jnp.add, [slices[c] * factors[c] for c in range(N)])
    for o in order:
        me_copy(o).start()

    for t in range(1, HOPS + 1):
        for p in range(2):
            two_copy(t - 1, p, ring(z + 2 * t)).wait_recv()
            if t < HOPS:
                two_copy(t, p, ring(z + 2 * t)).start()
                one_copy(t, p, ring(z + 2 * t)).start()
            up_copy(t - 1, p, ring(z - t)).wait_recv()
            if t < HOPS:
                up_copy(t, p, ring(z - t)).start()
        a_step(2)
        for p in range(2):
            one_copy(t - 1, p, ring(z + 2 * t - 1)).wait_recv()
        lost_pieces([ring(z + 2 * t - 1), ring(z + 2 * t), ring(z - t)])
    for o in order:
        me_copy(o).wait_recv()

    tops = [top_fresh, lost["top"], top_alive]
    totals = [total_fresh, lost["total"], total_alive]
    top = functools.reduce(jnp.maximum, tops)
    factors = [jnp.exp(v - top) for v in tops]
    total = functools.reduce(jnp.add, [v * f for v, f in zip(totals, factors)])
    mix = mix_fresh * factors[0] + lost_mix[...] * factors[1]
    mix = mix + jnp.concatenate([merged[c] for c in range(N)], axis=0) * factors[2]
    att[...] = jnp.transpose(mix / total).astype(BF16)
    log_row = top + jnp.log(total)
    for n in range(8):
        turned = log_row if n == 0 else pltpu.roll(log_row, HD - 16 * n, 1)
        logs[n // 4, n % 4:n % 4 + 1, :] = turned[:, :16]

    @pl.when(z != 0)
    def _():
        for n in range(A_PARTS):
            a_copy(n).wait_recv()

    for p in range(2):
        for b in range(BLOCKS):
            tiles = [msgs[c, p, b * 16:(b + 1) * 16, :].astype(F32) for c in range(N)]
            rows = slice(b * BLK, (b + 1) * BLK)
            for s in range(2):
                rebuilt = jnp.concatenate([tile[s * SUB:(s + 1) * SUB] for tile in tiles], axis=0)
                ext[2 * p + s, rows, :] = jnp.where(z - 1 == fc, rebuilt, lower[2 * p + s, rows, :].astype(F32))
    for seq in range(2):
        begin = jnp.int32(0)
        length = jnp.int32(0)
        for j in range(N - 1):
            size = lengths[seq, j]
            begin = begin + jnp.where(j < z - 1, size, 0)
            length = jnp.where(j == z - 1, size, length)
        offset = jnp.clip(begin - (z - 1) * CTX, 0, CTX)
        slot = iota((PIECE, HD), 0)
        for p in range(2):
            for n in range(CAP // PIECE):
                rows = ext[2 * p + seq, pl.ds(offset + n * PIECE, PIECE), :]
                rows = jnp.where(slot + n * PIECE < length, rows, 0.0)
                out[2 * p + seq, n * PIECE:(n + 1) * PIECE, :] = rows.astype(BF16)

    for o in order:
        for make in (b_copy, s_copy, st_copy, sl_copy, me_copy):
            make(o).wait_send()
    for p in range(2):
        for j in range(MP):
            x_copy(j, p, k).wait_send()
        for t in range(HOPS):
            two_copy(t, p, ring(z + 2 * t)).wait_send()
            one_copy(t, p, ring(z + 2 * t)).wait_send()
            up_copy(t, p, ring(z - t)).wait_send()

    @pl.when(z != N - 1)
    def _():
        for n in range(A_PARTS):
            a_copy(n).wait_send()


def restore(slots, *operands):
    vmem = pl.BlockSpec(memory_space=pltpu.VMEM)
    hbm = pl.BlockSpec(memory_space=pltpu.HBM)
    dma = pltpu.SemaphoreType.DMA
    return pl.pallas_call(
        functools.partial(kernel, slots),
        out_shape=(
            jax.ShapeDtypeStruct((4, CAP, HD), BF16),
            jax.ShapeDtypeStruct((HD, HD), BF16),
            jax.ShapeDtypeStruct((2, 4, 16), F32),
        ),
        in_specs=[hbm] * 8,
        out_specs=(vmem, vmem, vmem),
        scratch_shapes=[
            pltpu.VMEM((4, CTX, HD), BF16),
            pltpu.VMEM((4, CTX, HD), BF16),
            pltpu.VMEM((2, 2, BLOCKS), BF16),
            pltpu.SMEM((BLOCKS,), jnp.int32),
            pltpu.SMEM((1,), jnp.int32),
            pltpu.SMEM((2, N - 1), jnp.int32),
            pltpu.VMEM((HD, HD), BF16),
            pltpu.VMEM((16, HD), BF16),
            pltpu.VMEM((4, CTX, HD), BF16),
            pltpu.VMEM((N, slots, 2, 16, HD), BF16),
            pltpu.VMEM((N, slots, 2, 16, HD), BF16),
            pltpu.VMEM((N, 1, HD), F32),
            pltpu.VMEM((2, PACK, HD), BF16),
            pltpu.VMEM((2, MP, PACK, HD), BF16),
            pltpu.VMEM((N, 2, ROWS, HD), BF16),
            pltpu.VMEM((CTX, HD), F32),
            pltpu.VMEM((HD, HD), F32),
            pltpu.VMEM((N, 2, 1, HD), F32),
            pltpu.VMEM((N, SUB, HD), F32),
            pltpu.VMEM((N, SUB, HD), F32),
            pltpu.VMEM((HD, HD), F32),
            pltpu.VMEM((4, CTX + CAP, HD), F32),
            dma((8,)),
            dma((A_PARTS,)), dma((A_PARTS,)),
            dma((N,)), dma((N,)), dma((N,)), dma((N,)),
            dma((MP, 2)), dma((MP, 2)),
            dma((HOPS, 2)), dma((HOPS, 2)),
            dma((HOPS, 2)), dma((HOPS, 2)),
            dma((HOPS, 2)), dma((HOPS, 2)),
            dma((N,)), dma((N,)), dma((N,)), dma((N,)), dma((N,)), dma((N,)),
        ],
        compiler_params=pltpu.CompilerParams(
            collective_id=slots, has_side_effects=True, vmem_limit_bytes=56 * 1024 * 1024),
        cost_estimate=pl.CostEstimate(flops=10**8, bytes_accessed=4 * 10**6, transcendentals=2 * 10**5),
    )(*operands)


SLOTS = (2, 3, 8)


def body(kv_cache, backup_codes, backup_scales, block_shift, failed, new_lengths, queries, new_kv):
    most = jnp.max(jnp.sum((block_shift[:, None] == block_shift[None, :]).astype(jnp.int32), axis=1))
    branch = (most > 2).astype(jnp.int32) + (most > 3).astype(jnp.int32)
    out, att, logs = lax.switch(
        branch,
        [functools.partial(restore, slots) for slots in SLOTS],
        kv_cache.reshape(4, CTX, HD),
        backup_codes.reshape(4, CTX, HD),
        backup_scales.reshape(2, 2, BLOCKS),
        block_shift,
        failed,
        new_lengths,
        queries.reshape(HD, HD),
        new_kv.reshape(16, HD),
    )
    return (
        out.reshape(2, 2, CAP, 1, HD),
        att.reshape(queries.shape),
        logs,
    )


def solution(mesh):
    return jax.shard_map(
        body,
        mesh=mesh,
        in_specs=(
            P(None, "batch", "ctx", "mp", None),
            P(None, "batch", "ctx", "mp", None),
            P(None, "batch", "ctx", "mp"),
            P(),
            P(),
            P("batch", None),
            P("batch", None, "mp", None),
            P(None, "batch", None, "mp", None),
        ),
        out_specs=(
            P(None, "batch", "ctx", "mp", None),
            P("batch", None, "mp", None),
            P("batch", None, "mp"),
        ),
        check_vma=False,
    )
```

```python
import functools
import math

import jax
import jax.numpy as jnp
from jax import lax
from jax.experimental import pallas as pl
from jax.experimental.pallas import tpu as pltpu
from jax.sharding import PartitionSpec as P

F32 = jnp.float32
BF16 = jnp.bfloat16
MESH = pl.DeviceIdType.MESH

far_below = -1e30

BLK = 128
N = 16
NB = 8
MP = 4
HD = 128
CTX = 1024
CAP = 1216
PIECE = CTX // N
ROWS = 2 * PIECE
PACK = ROWS + 16
BLOCKS = CTX // BLK
SUB = 8

HOPS = 5
A_PARTS = 16


def dot_tt(a, b):
    return lax.dot_general(a, b, (((1,), (1,)), ((), ())), preferred_element_type=F32)


def dot_sum_rows(a, b):
    return lax.dot_general(a, b, (((0,), (0,)), ((), ())), preferred_element_type=F32)


def iota(shape, dim):
    return lax.broadcasted_iota(jnp.int32, shape, dim)


def kernel(slots, kv_hbm, codes_hbm, scales_hbm, shift_hbm, failed_hbm, lengths_hbm, q_hbm, fresh_hbm,
           out, att, logs,
           kv, codes, scales, shift, failed, lengths, q, fresh,
           lower, bsend, bbuf, srow, xsend, xbuf, msgs, score, own_mix, sent_mix, stats, slices, merged, lost_mix, ext,
           in_sem, a_send, a_recv, b_send, b_recv, s_send, s_recv, x_send, x_recv,
           one_send, one_recv, two_send, two_recv, up_send, up_recv,
           st_send, st_recv, sl_send, sl_recv, me_send, me_recv):
    z = lax.axis_index("ctx")
    g = lax.axis_index("batch")
    k = lax.axis_index("mp")

    fetch = [
        pltpu.make_async_copy(source, target, in_sem.at[n])
        for n, (source, target) in enumerate((
            (codes_hbm, codes), (failed_hbm, failed), (shift_hbm, shift), (scales_hbm, scales),
            (kv_hbm, kv), (q_hbm, q), (fresh_hbm, fresh), (lengths_hbm, lengths)))
    ]
    for copy in fetch:
        copy.start()

    def ring(c):
        return lax.rem(c + 2 * N, N)

    g_to, g_from = lax.rem(g + NB - 1, NB), lax.rem(g + 1, NB)

    barrier = pltpu.get_barrier_semaphore()
    for o in range(1, N):
        pl.semaphore_signal(barrier, inc=1, device_id=(ring(z + o), g, k), device_id_type=MESH)
    for j in range(MP):
        pl.semaphore_signal(barrier, inc=1, device_id=(z, g_to, j), device_id_type=MESH)
        pl.semaphore_signal(barrier, inc=1, device_id=(z, g_from, j), device_id_type=MESH)

    for copy in fetch[:4]:
        copy.wait()
    fc = lax.rem(failed[0], N)
    lane = iota((16, HD), 1)
    row = iota((16, HD), 0)

    shifts = [shift[b] for b in range(BLOCKS)]
    holder = [lax.rem(fc + v, N) for v in shifts]
    rank = []
    for b in range(BLOCKS):
        before = jnp.int32(0)
        for e in range(b):
            before = before + jnp.where(shifts[e] == shifts[b], 1, 0)
        rank.append(jnp.minimum(before, slots - 1))
    def chosen(b, h, j):
        return (holder[b] == h) & (rank[b] == j)

    for j in range(slots):
        for p in range(2):
            pair = []
            for s in range(2):
                block = codes[2 * p + s, j * BLK:(j + 1) * BLK, :]
                for b in range(j + 1, BLOCKS):
                    block = jnp.where(chosen(b, z, j), codes[2 * p + s, b * BLK:(b + 1) * BLK, :], block)
                pair.append(block.astype(F32))
            for c in range(N):
                part = slice(c * SUB, (c + 1) * SUB)
                bsend[c, j, p] = jnp.concatenate([pair[0][part], pair[1][part]], axis=0).astype(BF16)
    line = jnp.zeros((1, HD), F32)
    for p in range(2):
        both = scales[p].astype(F32)
        for s in range(2):
            wide = jnp.concatenate([both[s:s + 1], jnp.zeros((1, HD - BLOCKS), F32)], axis=1)
            at = (2 * p + s) * BLOCKS
            line = line + (pltpu.roll(wide, at, 1) if at else wide)
    srow[z] = line
    bbuf[z] = bsend[z]

    def peer_copy(o, source, target, send, recv):
        return pltpu.make_async_remote_copy(
            src_ref=source, dst_ref=target, send_sem=send.at[o], recv_sem=recv.at[o],
            device_id=(ring(z + o), g, k), device_id_type=MESH)

    def b_copy(o):
        return peer_copy(o, bsend.at[ring(z + o)], bbuf.at[z], b_send, b_recv)

    def s_copy(o):
        return peer_copy(o, srow.at[z], srow.at[z], s_send, s_recv)

    def st_copy(o):
        return peer_copy(o, stats.at[z], stats.at[z], st_send, st_recv)

    def sl_copy(i, source):
        return pltpu.make_async_remote_copy(
            src_ref=sent_mix.at[i], dst_ref=slices.at[source], send_sem=sl_send.at[i], recv_sem=sl_recv.at[source],
            device_id=(2 * i, g, k), device_id_type=MESH)

    def me_copy(o, i):
        return pltpu.make_async_remote_copy(
            src_ref=merged.at[i], dst_ref=merged.at[i], send_sem=me_send.at[o], recv_sem=me_recv.at[i],
            device_id=(ring(z + o), g, k), device_id_type=MESH)

    merging = lax.rem(z, 2) == 0
    my_slice = z // 2

    order = [8, 7, 9, 6, 10, 5, 11, 4, 12, 3, 13, 2, 14, 1, 15]
    pl.semaphore_wait(barrier, N - 1 + 2 * MP)
    for o in order:
        b_copy(o).start()
        s_copy(o).start()

    def a_copy(n):
        rows = slice(n * (CTX // A_PARTS), (n + 1) * (CTX // A_PARTS))
        return pltpu.make_async_remote_copy(
            src_ref=kv.at[:, rows, :], dst_ref=lower.at[:, rows, :], send_sem=a_send.at[n], recv_sem=a_recv.at[n],
            device_id=(ring(z + 1), g, k), device_id_type=MESH)

    a_started = [0]

    def a_step(count):
        first = a_started[0]
        last = min(first + count, A_PARTS)
        a_started[0] = last

        @pl.when(z != N - 1)
        def _():
            for n in range(first, last):
                a_copy(n).start()

    for copy in fetch[4:]:
        copy.wait()

    half = iota((HD, HD), 0) < HD // 2
    queries = q[...]
    zero = jnp.zeros((HD, HD), BF16)
    q0, q1 = jnp.where(half, queries, zero), jnp.where(half, zero, queries)
    first_half = iota((1, HD), 1) < HD // 2
    scaling = 1.0 / math.sqrt(HD)
    alive = z != fc
    CH = 256

    top_own = jnp.full((1, HD), far_below, F32)
    for n in range(CTX // CH):
        rows = slice(n * CH, (n + 1) * CH)
        s = (dot_tt(kv[0, rows, :], q0) + dot_tt(kv[1, rows, :], q1)) * scaling
        s = jnp.where(alive, s, far_below)
        score[rows, :] = s
        top_own = jnp.maximum(top_own, jnp.max(s, axis=0, keepdims=True))
    total_own = jnp.zeros((1, HD), F32)
    for n in range(CTX // CH):
        rows = slice(n * CH, (n + 1) * CH)
        w = jnp.where(alive, jnp.exp(score[rows, :] - top_own), 0.0)
        total_own = total_own + jnp.sum(w, axis=0, keepdims=True)
        w0 = jnp.where(first_half, w, 0.0).astype(BF16)
        w1 = jnp.where(first_half, 0.0, w).astype(BF16)
        mix = dot_sum_rows(kv[2, rows, :], w0) + dot_sum_rows(kv[3, rows, :], w1)
        own_mix[...] = mix if n == 0 else own_mix[...] + mix
    stats[z, 0] = top_own
    stats[z, 1] = total_own
    for i in range(N // 2):
        sent_mix[i] = own_mix[16 * i:16 * i + 16, :].astype(BF16)
    slices[z] = sent_mix[my_slice]

    fresh_rows = fresh[...]
    s = dot_tt(fresh_rows, queries) * scaling
    usable = (row < 8) & (row // 4 == lane // 64) & (lax.rem(row, 4) <= lax.rem(lane, 64) // 16)
    s = jnp.where(usable, s, far_below)
    top_fresh = jnp.max(s, axis=0, keepdims=True)
    w = jnp.where(usable, jnp.exp(s - top_fresh), 0.0)
    total_fresh = jnp.sum(w, axis=0, keepdims=True)
    w = jnp.concatenate([jnp.zeros((8, HD), F32), w[:8]], axis=0).astype(BF16)
    mix_fresh = dot_sum_rows(fresh_rows, w)

    shared = iota((HD, HD), 0) & iota((HD, HD), 1)
    shared = shared ^ (shared >> 4)
    shared = shared ^ (shared >> 2)
    shared = (shared ^ (shared >> 1)) & 1
    signs = (1 - 2 * shared).astype(F32).astype(BF16)

    for i in range(4):
        for n in range(CTX // CH):
            ext[i, CTX + n * CH:CTX + (n + 1) * CH, :] = kv[i, n * CH:(n + 1) * CH, :].astype(F32)
        ext[i, 2 * CTX:, :] = jnp.zeros((CAP - CTX, HD), F32)

    for o in order:
        b_copy(o).wait_recv()
        s_copy(o).wait_recv()
    tiles = [jnp.zeros((16, HD), F32) for _ in range(2)]
    for b in range(BLOCKS):
        line = srow[0]
        for h in range(1, N):
            line = jnp.where(holder[b] == h, srow[h], line)
        for p in range(2):
            for s in range(2):
                at = (2 * p + s) * BLOCKS + b
                tiles[p] = jnp.where(row == 2 * b + s, line[:, at:at + 1], tiles[p])

    def x_copy(j, p, slot):
        return pltpu.make_async_remote_copy(
            src_ref=xsend.at[p], dst_ref=xbuf.at[p, slot],
            send_sem=x_send.at[j, p], recv_sem=x_recv.at[slot, p],
            device_id=(z, g_to, j), device_id_type=MESH)

    for p in range(2):
        for b in range(BLOCKS):
            tile = bbuf[0, 0, p]
            for h in range(N):
                for j in range(min(slots, b + 1)):
                    if h + j > 0:
                        tile = jnp.where(chosen(b, h, j), bbuf[h, j, p], tile)
            xsend[p, b * 16:(b + 1) * 16, :] = tile
        xsend[p, ROWS:, :] = tiles[p].astype(BF16)
        for j in range(MP):
            x_copy(j, p, k).start()
    for o in order:
        st_copy(o).start()
    for i in range(N // 2):
        @pl.when(z != 2 * i)
        def _():
            sl_copy(i, z).start()
    a_step(7)

    def one_copy(t, p, piece):
        return pltpu.make_async_remote_copy(
            src_ref=msgs.at[piece, p], dst_ref=msgs.at[piece, p], send_sem=one_send.at[t, p], recv_sem=one_recv.at[t, p],
            device_id=(ring(z - 1), g, k), device_id_type=MESH)

    def two_copy(t, p, piece):
        return pltpu.make_async_remote_copy(
            src_ref=msgs.at[piece, p], dst_ref=msgs.at[piece, p], send_sem=two_send.at[t, p], recv_sem=two_recv.at[t, p],
            device_id=(ring(z - 2), g, k), device_id_type=MESH)

    def up_copy(t, p, piece):
        return pltpu.make_async_remote_copy(
            src_ref=msgs.at[piece, p], dst_ref=msgs.at[piece, p], send_sem=up_send.at[t, p], recv_sem=up_recv.at[t, p],
            device_id=(ring(z + 1), g, k), device_id_type=MESH)

    norm = 1.0 / math.sqrt(MP * HD)
    for p in range(2):
        mixed = None
        for j in range(MP):
            x_copy(j, p, j).wait_recv()
            common = k & j
            odd = (common ^ (common >> 1)) & 1
            coef = jnp.where(odd == 1, -norm, norm).astype(F32)
            tile = xbuf[p, j, ROWS:, :].astype(F32)
            wide = jnp.concatenate([jnp.broadcast_to(tile[r:r + 1], (SUB, HD)) for r in range(16)], axis=0)
            term = jnp.dot(xbuf[p, j, :ROWS, :], signs, preferred_element_type=F32) * wide * coef
            mixed = term if j == 0 else mixed + term
        msgs[z, p] = mixed.astype(BF16)
        two_copy(0, p, z).start()
        up_copy(0, p, z).start()
        one_copy(0, p, z).start()

    lost = {}

    def lost_pieces(pieces):
        count = len(pieces)
        keys = jnp.concatenate([msgs[c, 0] for c in pieces], axis=0)
        values = jnp.concatenate([msgs[c, 1] for c in pieces], axis=0)
        matching = ((iota((ROWS * count, HD), 0) // SUB) & 1) == iota((ROWS * count, HD), 1) // (HD // 2)
        s = jnp.where(matching, dot_tt(keys, queries) * scaling, far_below)
        top = jnp.max(s, axis=0, keepdims=True)
        if lost:
            top = jnp.maximum(top, lost["top"])
        w = jnp.where(matching, jnp.exp(s - top), 0.0)
        total = jnp.sum(w, axis=0, keepdims=True)
        mix = dot_sum_rows(values, w.astype(BF16))
        if lost:
            factor = jnp.exp(lost["top"] - top)
            total = total + lost["total"] * factor
            mix = mix + lost_mix[...] * factor
        lost_mix[...] = mix
        lost["top"], lost["total"] = top, total
        for c in pieces:
            for p in range(2):
                for b in range(BLOCKS):
                    tile = msgs[c, p, b * 16:(b + 1) * 16, :].astype(F32)
                    below = pl.ds(pl.multiple_of(b * BLK + c * SUB, SUB), SUB)
                    here = pl.ds(pl.multiple_of(CTX + b * BLK + c * SUB, SUB), SUB)
                    for s in range(2):
                        rebuilt = tile[s * SUB:(s + 1) * SUB]
                        ext[2 * p + s, here, :] = jnp.where(z == fc, rebuilt, ext[2 * p + s, here, :])
                        ext[2 * p + s, below, :] = jnp.where(z - 1 == fc, rebuilt, ext[2 * p + s, below, :])

    a_step(3)
    lost_pieces([z])

    for o in order:
        st_copy(o).wait_recv()
    tops = [stats[c, 0] for c in range(N)]
    top_alive = functools.reduce(jnp.maximum, tops)
    factors = [jnp.exp(v - top_alive) for v in tops]
    total_alive = functools.reduce(jnp.add, [stats[c, 1] * factors[c] for c in range(N)])

    @pl.when(merging)
    def _():
        for c in range(N):
            @pl.when(z != c)
            def _():
                sl_copy(0, c).wait_recv()
        total_mix = functools.reduce(jnp.add, [slices[c].astype(F32) * factors[c] for c in range(N)])
        merged[my_slice] = total_mix.astype(BF16)
        for o in order:
            me_copy(o, my_slice).start()

    lost_below = z - 1 == fc

    def lower_parts(first, last):
        @pl.when(z != 0)
        def _():
            for n in range(first, last):
                a_copy(n).wait_recv()

        for n in range(first, last):
            rows = slice(n * (CTX // A_PARTS), (n + 1) * (CTX // A_PARTS))
            for i in range(4):
                ext[i, rows, :] = jnp.where(lost_below, ext[i, rows, :], lower[i, rows, :].astype(F32))

    lower_at = {2: (0, 5), 3: (5, 9), 4: (9, 11), 5: (11, 14)}
    for t in range(1, HOPS + 1):
        for p in range(2):
            two_copy(t - 1, p, ring(z + 2 * t)).wait_recv()
            if t < HOPS:
                two_copy(t, p, ring(z + 2 * t)).start()
                one_copy(t, p, ring(z + 2 * t)).start()
            up_copy(t - 1, p, ring(z - t)).wait_recv()
            if t < HOPS:
                up_copy(t, p, ring(z - t)).start()
        a_step(2)
        if t >= 2:
            lower_parts(*lower_at[t])
        for p in range(2):
            one_copy(t - 1, p, ring(z + 2 * t - 1)).wait_recv()
        lost_pieces([ring(z + 2 * t - 1), ring(z + 2 * t), ring(z - t)])
    for i in range(N // 2):
        @pl.when(z != 2 * i)
        def _():
            me_copy(1, i).wait_recv()

    tops = [top_fresh, lost["top"], top_alive]
    totals = [total_fresh, lost["total"], total_alive]
    top = functools.reduce(jnp.maximum, tops)
    factors = [jnp.exp(v - top) for v in tops]
    total = functools.reduce(jnp.add, [v * f for v, f in zip(totals, factors)])
    mix = mix_fresh * factors[0] + lost_mix[...] * factors[1]
    mix = mix + jnp.concatenate([merged[i].astype(F32) for i in range(N // 2)], axis=0) * factors[2]
    att[...] = jnp.transpose(mix / total).astype(BF16)
    log_row = top + jnp.log(total)
    for n in range(8):
        turned = log_row if n == 0 else pltpu.roll(log_row, HD - 16 * n, 1)
        logs[n // 4, n % 4:n % 4 + 1, :] = turned[:, :16]

    lower_parts(14, A_PARTS)
    for seq in range(2):
        begin = jnp.int32(0)
        length = jnp.int32(0)
        for j in range(N - 1):
            size = lengths[seq, j]
            begin = begin + jnp.where(j < z - 1, size, 0)
            length = jnp.where(j == z - 1, size, length)
        offset = jnp.clip(begin - (z - 1) * CTX, 0, CTX)
        slot = iota((PIECE, HD), 0)
        for p in range(2):
            for n in range(CAP // PIECE):
                rows = ext[2 * p + seq, pl.ds(offset + n * PIECE, PIECE), :]
                rows = jnp.where(slot + n * PIECE < length, rows, 0.0)
                out[2 * p + seq, n * PIECE:(n + 1) * PIECE, :] = rows.astype(BF16)

    for o in order:
        for make in (b_copy, s_copy, st_copy):
            make(o).wait_send()
    for i in range(N // 2):
        @pl.when(z != 2 * i)
        def _():
            sl_copy(i, z).wait_send()

    @pl.when(merging)
    def _():
        for o in order:
            me_copy(o, my_slice).wait_send()

    for p in range(2):
        for j in range(MP):
            x_copy(j, p, k).wait_send()
        for t in range(HOPS):
            two_copy(t, p, ring(z + 2 * t)).wait_send()
            one_copy(t, p, ring(z + 2 * t)).wait_send()
            up_copy(t, p, ring(z - t)).wait_send()

    @pl.when(z != N - 1)
    def _():
        for n in range(A_PARTS):
            a_copy(n).wait_send()


def restore(slots, *operands):
    vmem = pl.BlockSpec(memory_space=pltpu.VMEM)
    hbm = pl.BlockSpec(memory_space=pltpu.HBM)
    dma = pltpu.SemaphoreType.DMA
    return pl.pallas_call(
        functools.partial(kernel, slots),
        out_shape=(
            jax.ShapeDtypeStruct((4, CAP, HD), BF16),
            jax.ShapeDtypeStruct((HD, HD), BF16),
            jax.ShapeDtypeStruct((2, 4, 16), F32),
        ),
        in_specs=[hbm] * 8,
        out_specs=(vmem, vmem, vmem),
        scratch_shapes=[
            pltpu.VMEM((4, CTX, HD), BF16),
            pltpu.VMEM((4, CTX, HD), BF16),
            pltpu.VMEM((2, 2, BLOCKS), BF16),
            pltpu.SMEM((BLOCKS,), jnp.int32),
            pltpu.SMEM((1,), jnp.int32),
            pltpu.SMEM((2, N - 1), jnp.int32),
            pltpu.VMEM((HD, HD), BF16),
            pltpu.VMEM((16, HD), BF16),
            pltpu.VMEM((4, CTX, HD), BF16),
            pltpu.VMEM((N, slots, 2, 16, HD), BF16),
            pltpu.VMEM((N, slots, 2, 16, HD), BF16),
            pltpu.VMEM((N, 1, HD), F32),
            pltpu.VMEM((2, PACK, HD), BF16),
            pltpu.VMEM((2, MP, PACK, HD), BF16),
            pltpu.VMEM((N, 2, ROWS, HD), BF16),
            pltpu.VMEM((CTX, HD), F32),
            pltpu.VMEM((HD, HD), F32),
            pltpu.VMEM((N // 2, 16, HD), BF16),
            pltpu.VMEM((N, 2, 1, HD), F32),
            pltpu.VMEM((N, 16, HD), BF16),
            pltpu.VMEM((N // 2, 16, HD), BF16),
            pltpu.VMEM((HD, HD), F32),
            pltpu.VMEM((4, CTX + CAP, HD), F32),
            dma((8,)),
            dma((A_PARTS,)), dma((A_PARTS,)),
            dma((N,)), dma((N,)), dma((N,)), dma((N,)),
            dma((MP, 2)), dma((MP, 2)),
            dma((HOPS, 2)), dma((HOPS, 2)),
            dma((HOPS, 2)), dma((HOPS, 2)),
            dma((HOPS, 2)), dma((HOPS, 2)),
            dma((N,)), dma((N,)), dma((N,)), dma((N,)), dma((N,)), dma((N,)),
        ],
        compiler_params=pltpu.CompilerParams(
            collective_id=slots, has_side_effects=True, vmem_limit_bytes=56 * 1024 * 1024),
        cost_estimate=pl.CostEstimate(flops=10**8, bytes_accessed=4 * 10**6, transcendentals=2 * 10**5),
    )(*operands)


SLOTS = (2, 3, 8)


def body(kv_cache, backup_codes, backup_scales, block_shift, failed, new_lengths, queries, new_kv):
    cube = (BLOCKS,) * 3
    ids = [lax.broadcasted_iota(jnp.int32, cube, n) for n in range(3)]
    spread = [lax.broadcast_in_dim(block_shift, cube, (n,)) for n in range(3)]
    equal = (spread[0] == spread[1]) & (spread[1] == spread[2]) & (ids[0] < ids[1]) & (ids[1] < ids[2])
    triples = jnp.sum(equal.astype(jnp.int32))
    branch = (triples > 0).astype(jnp.int32) + (triples > 3).astype(jnp.int32)
    out, att, logs = lax.switch(
        branch,
        [functools.partial(restore, slots) for slots in SLOTS],
        kv_cache.reshape(4, CTX, HD),
        backup_codes.reshape(4, CTX, HD),
        backup_scales.reshape(2, 2, BLOCKS),
        block_shift,
        failed,
        new_lengths,
        queries.reshape(HD, HD),
        new_kv.reshape(16, HD),
    )
    return (
        out.reshape(2, 2, CAP, 1, HD),
        att.reshape(queries.shape),
        logs,
    )


def solution(mesh):
    return jax.shard_map(
        body,
        mesh=mesh,
        in_specs=(
            P(None, "batch", "ctx", "mp", None),
            P(None, "batch", "ctx", "mp", None),
            P(None, "batch", "ctx", "mp"),
            P(),
            P(),
            P("batch", None),
            P("batch", None, "mp", None),
            P(None, "batch", None, "mp", None),
        ),
        out_specs=(
            P(None, "batch", "ctx", "mp", None),
            P("batch", None, "mp", None),
            P("batch", None, "mp"),
        ),
        check_vma=False,
    )
```

```python
import functools
import math

import jax
import jax.numpy as jnp
from jax import lax
from jax.experimental import pallas as pl
from jax.experimental.pallas import tpu as pltpu
from jax.sharding import PartitionSpec as P

F32 = jnp.float32
BF16 = jnp.bfloat16
MESH = pl.DeviceIdType.MESH

far_below = -1e30

BLK = 128
N = 16
NB = 8
MP = 4
HD = 128
CTX = 1024
CAP = 1216
PIECE = CTX // N
ROWS = 2 * PIECE
PACK = ROWS + 16
BLOCKS = CTX // BLK
SUB = 8

HOPS = 5
A_PARTS = 8


def dot_tt(a, b):
    return lax.dot_general(a, b, (((1,), (1,)), ((), ())), preferred_element_type=F32)


def dot_sum_rows(a, b):
    return lax.dot_general(a, b, (((0,), (0,)), ((), ())), preferred_element_type=F32)


def iota(shape, dim):
    return lax.broadcasted_iota(jnp.int32, shape, dim)


def split_three(x):
    hi = x.astype(BF16).astype(F32)
    rest = x - hi
    mid = rest.astype(BF16).astype(F32)
    return hi, mid, rest - mid


def stat_tile(row, top, total):
    tile = jnp.zeros((16, HD), F32)
    for n, piece in enumerate(split_three(top) + split_three(total)):
        tile = jnp.where(row == n, piece, tile)
    return tile.astype(BF16)


def stat_rows(tile):
    tile = tile.astype(F32)
    return tile[0:1] + tile[1:2] + tile[2:3], tile[3:4] + tile[4:5] + tile[5:6]


def kernel(slots, kv_hbm, codes_hbm, scales_hbm, shift_hbm, failed_hbm, lengths_hbm, q_hbm, fresh_hbm,
           out, att, logs,
           kv, codes, scales, shift, failed, lengths, q, fresh,
           lower, bsend, bbuf, srow, xsend, xbuf, msgs, score, own_mix, sent_mix, slices, merged, all_mix, lost_mix, ext,
           in_sem, a_send, a_recv, b_send, b_recv, s_send, s_recv, x_send, x_recv,
           one_recv, two_recv, up_recv, g_send, sl_send, sl_recv, me_send, me_recv):
    z = lax.axis_index("ctx")
    g = lax.axis_index("batch")
    k = lax.axis_index("mp")

    fetch = [
        pltpu.make_async_copy(source, target, in_sem.at[n])
        for n, (source, target) in enumerate((
            (codes_hbm, codes), (failed_hbm, failed), (shift_hbm, shift), (scales_hbm, scales),
            (kv_hbm, kv), (q_hbm, q), (fresh_hbm, fresh), (lengths_hbm, lengths)))
    ]
    for copy in fetch:
        copy.start()

    def ring(c):
        return lax.rem(c + 2 * N, N)

    g_to, g_from = lax.rem(g + NB - 1, NB), lax.rem(g + 1, NB)

    barrier = pltpu.get_barrier_semaphore()
    for o in range(1, N):
        pl.semaphore_signal(barrier, inc=1, device_id=(ring(z + o), g, k), device_id_type=MESH)
    for j in range(MP):
        pl.semaphore_signal(barrier, inc=1, device_id=(z, g_to, j), device_id_type=MESH)
        pl.semaphore_signal(barrier, inc=1, device_id=(z, g_from, j), device_id_type=MESH)

    for copy in fetch[:4]:
        copy.wait()
    fc = lax.rem(failed[0], N)
    lane = iota((16, HD), 1)
    row = iota((16, HD), 0)

    shifts = [shift[b] for b in range(BLOCKS)]
    holder = [lax.rem(fc + v, N) for v in shifts]
    rank = []
    for b in range(BLOCKS):
        before = jnp.int32(0)
        for e in range(b):
            before = before + jnp.where(shifts[e] == shifts[b], 1, 0)
        rank.append(jnp.minimum(before, slots - 1))
    def chosen(b, h, j):
        return (holder[b] == h) & (rank[b] == j)

    for j in range(slots):
        for p in range(2):
            pair = []
            for s in range(2):
                block = codes[2 * p + s, j * BLK:(j + 1) * BLK, :]
                for b in range(j + 1, BLOCKS):
                    block = jnp.where(chosen(b, z, j), codes[2 * p + s, b * BLK:(b + 1) * BLK, :], block)
                pair.append(block.astype(F32))
            for c in range(N):
                part = slice(c * SUB, (c + 1) * SUB)
                bsend[c, j, p] = jnp.concatenate([pair[0][part], pair[1][part]], axis=0).astype(BF16)
    line = jnp.zeros((1, HD), F32)
    for p in range(2):
        both = scales[p].astype(F32)
        for s in range(2):
            wide = jnp.concatenate([both[s:s + 1], jnp.zeros((1, HD - BLOCKS), F32)], axis=1)
            at = (2 * p + s) * BLOCKS
            line = line + (pltpu.roll(wide, at, 1) if at else wide)
    srow[N - 1] = line
    bbuf[N - 1] = bsend[z]

    def peer_copy(o, source, target, send, recv):
        return pltpu.make_async_remote_copy(
            src_ref=source, dst_ref=target, send_sem=send, recv_sem=recv,
            device_id=(ring(z + o), g, k), device_id_type=MESH)

    def b_copy(o):
        return peer_copy(o, bsend.at[ring(z + o)], bbuf.at[o - 1], b_send, b_recv)

    def s_copy(o):
        return peer_copy(o, srow.at[N - 1], srow.at[o - 1], s_send, s_recv)

    def sl_copy(o):
        return peer_copy(o, sent_mix.at[ring(z + o) // 2], slices.at[o - 1], sl_send, sl_recv)

    def me_copy(o):
        return peer_copy(o, merged.at[N // 2 - 1], merged.at[(o - 1) // 2], me_send, me_recv)

    def whole(ref, send, recv):
        return peer_copy(1, ref, ref, send, recv)

    even, odd = range(2, N, 2), range(1, N, 2)
    merging = lax.rem(z, 2) == 0
    my_slice = z // 2

    order = [8, 7, 9, 6, 10, 5, 11, 4, 12, 3, 13, 2, 14, 1, 15]
    pl.semaphore_wait(barrier, N - 1 + 2 * MP)
    for o in order:
        b_copy(o).start()
        s_copy(o).start()

    def a_copy(n):
        rows = slice(n * (CTX // A_PARTS), (n + 1) * (CTX // A_PARTS))
        return pltpu.make_async_remote_copy(
            src_ref=kv.at[:, rows, :], dst_ref=lower.at[:, rows, :], send_sem=a_send, recv_sem=a_recv.at[n],
            device_id=(ring(z + 1), g, k), device_id_type=MESH)

    a_started = [0]

    def a_step(count):
        first = a_started[0]
        last = min(first + count, A_PARTS)
        a_started[0] = last

        @pl.when(z != N - 1)
        def _():
            for n in range(first, last):
                a_copy(n).start()

    for copy in fetch[4:]:
        copy.wait()

    half = iota((HD, HD), 0) < HD // 2
    queries = q[...]
    zero = jnp.zeros((HD, HD), BF16)
    q0, q1 = jnp.where(half, queries, zero), jnp.where(half, zero, queries)
    first_half = iota((1, HD), 1) < HD // 2
    scaling = 1.0 / math.sqrt(HD)
    alive = z != fc
    CH = 256

    top_own = jnp.full((1, HD), far_below, F32)
    for n in range(CTX // CH):
        rows = slice(n * CH, (n + 1) * CH)
        s = (dot_tt(kv[0, rows, :], q0) + dot_tt(kv[1, rows, :], q1)) * scaling
        s = jnp.where(alive, s, far_below)
        score[rows, :] = s
        top_own = jnp.maximum(top_own, jnp.max(s, axis=0, keepdims=True))
    total_own = jnp.zeros((1, HD), F32)
    for n in range(CTX // CH):
        rows = slice(n * CH, (n + 1) * CH)
        w = jnp.where(alive, jnp.exp(score[rows, :] - top_own), 0.0)
        total_own = total_own + jnp.sum(w, axis=0, keepdims=True)
        w0 = jnp.where(first_half, w, 0.0).astype(BF16)
        w1 = jnp.where(first_half, 0.0, w).astype(BF16)
        mix = dot_sum_rows(kv[2, rows, :], w0) + dot_sum_rows(kv[3, rows, :], w1)
        own_mix[...] = mix if n == 0 else own_mix[...] + mix
    tile = stat_tile(row, top_own, total_own)
    for i in range(N // 2):
        sent_mix[i, :16, :] = own_mix[16 * i:16 * i + 16, :].astype(BF16)
        sent_mix[i, 16:, :] = tile
    slices[N - 1] = sent_mix[my_slice]

    fresh_rows = fresh[...]
    s = dot_tt(fresh_rows, queries) * scaling
    usable = (row < 8) & (row // 4 == lane // 64) & (lax.rem(row, 4) <= lax.rem(lane, 64) // 16)
    s = jnp.where(usable, s, far_below)
    top_fresh = jnp.max(s, axis=0, keepdims=True)
    w = jnp.where(usable, jnp.exp(s - top_fresh), 0.0)
    total_fresh = jnp.sum(w, axis=0, keepdims=True)
    w = jnp.concatenate([jnp.zeros((8, HD), F32), w[:8]], axis=0).astype(BF16)
    mix_fresh = dot_sum_rows(fresh_rows, w)

    shared = iota((HD, HD), 0) & iota((HD, HD), 1)
    shared = shared ^ (shared >> 4)
    shared = shared ^ (shared >> 2)
    shared = (shared ^ (shared >> 1)) & 1
    signs = (1 - 2 * shared).astype(F32).astype(BF16)

    for i in range(4):
        for n in range(CTX // CH):
            ext[i, CTX + n * CH:CTX + (n + 1) * CH, :] = kv[i, n * CH:(n + 1) * CH, :].astype(F32)
        ext[i, 2 * CTX:, :] = jnp.zeros((CAP - CTX, HD), F32)

    whole(bbuf.at[0:N - 1], b_send, b_recv).wait_recv()
    whole(srow.at[0:N - 1], s_send, s_recv).wait_recv()
    away = [ring(z - h) for h in holder]
    away = [jnp.where(v == 0, N - 1, v - 1) for v in away]
    tiles = [jnp.zeros((16, HD), F32) for _ in range(2)]
    for b in range(BLOCKS):
        line = srow[0]
        for h in range(1, N):
            line = jnp.where(away[b] == h, srow[h], line)
        for p in range(2):
            for s in range(2):
                at = (2 * p + s) * BLOCKS + b
                tiles[p] = jnp.where(row == 2 * b + s, line[:, at:at + 1], tiles[p])

    def x_copy(j, p, slot):
        return pltpu.make_async_remote_copy(
            src_ref=xsend.at[p], dst_ref=xbuf.at[p, slot],
            send_sem=x_send.at[p], recv_sem=x_recv.at[p],
            device_id=(z, g_to, j), device_id_type=MESH)

    for p in range(2):
        for b in range(BLOCKS):
            tile = bbuf[0, 0, p]
            for h in range(N):
                for j in range(min(slots, b + 1)):
                    if h + j > 0:
                        tile = jnp.where((away[b] == h) & (rank[b] == j), bbuf[h, j, p], tile)
            xsend[p, b * 16:(b + 1) * 16, :] = tile
        xsend[p, ROWS:, :] = tiles[p].astype(BF16)
        for j in range(MP):
            x_copy(j, p, k).start()
    @pl.when(merging)
    def _():
        for o in even:
            sl_copy(o).start()

    @pl.when(jnp.logical_not(merging))
    def _():
        for o in odd:
            sl_copy(o).start()

    a_step(3)

    def one_copy(t, p, piece):
        return pltpu.make_async_remote_copy(
            src_ref=msgs.at[piece, p], dst_ref=msgs.at[piece, p], send_sem=g_send, recv_sem=one_recv.at[t, p],
            device_id=(ring(z - 1), g, k), device_id_type=MESH)

    def two_copy(t, p, piece):
        return pltpu.make_async_remote_copy(
            src_ref=msgs.at[piece, p], dst_ref=msgs.at[piece, p], send_sem=g_send, recv_sem=two_recv.at[t, p],
            device_id=(ring(z - 2), g, k), device_id_type=MESH)

    def up_copy(t, p, piece):
        return pltpu.make_async_remote_copy(
            src_ref=msgs.at[piece, p], dst_ref=msgs.at[piece, p], send_sem=g_send, recv_sem=up_recv.at[t, p],
            device_id=(ring(z + 1), g, k), device_id_type=MESH)

    norm = 1.0 / math.sqrt(MP * HD)
    for p in range(2):
        mixed = None
        whole(xbuf.at[p], x_send.at[p], x_recv.at[p]).wait_recv()
        for j in range(MP):
            common = k & j
            odd = (common ^ (common >> 1)) & 1
            coef = jnp.where(odd == 1, -norm, norm).astype(F32)
            tile = xbuf[p, j, ROWS:, :].astype(F32)
            wide = jnp.concatenate([jnp.broadcast_to(tile[r:r + 1], (SUB, HD)) for r in range(16)], axis=0)
            term = jnp.dot(xbuf[p, j, :ROWS, :], signs, preferred_element_type=F32) * wide * coef
            mixed = term if j == 0 else mixed + term
        msgs[z, p] = mixed.astype(BF16)
        two_copy(0, p, z).start()
        up_copy(0, p, z).start()
        one_copy(0, p, z).start()

    lost = {}

    def lost_pieces(pieces):
        count = len(pieces)
        keys = jnp.concatenate([msgs[c, 0] for c in pieces], axis=0)
        values = jnp.concatenate([msgs[c, 1] for c in pieces], axis=0)
        matching = ((iota((ROWS * count, HD), 0) // SUB) & 1) == iota((ROWS * count, HD), 1) // (HD // 2)
        s = jnp.where(matching, dot_tt(keys, queries) * scaling, far_below)
        top = jnp.max(s, axis=0, keepdims=True)
        if lost:
            top = jnp.maximum(top, lost["top"])
        w = jnp.where(matching, jnp.exp(s - top), 0.0)
        total = jnp.sum(w, axis=0, keepdims=True)
        mix = dot_sum_rows(values, w.astype(BF16))
        if lost:
            factor = jnp.exp(lost["top"] - top)
            total = total + lost["total"] * factor
            mix = mix + lost_mix[...] * factor
        lost_mix[...] = mix
        lost["top"], lost["total"] = top, total
        for c in pieces:
            for p in range(2):
                for b in range(BLOCKS):
                    tile = msgs[c, p, b * 16:(b + 1) * 16, :].astype(F32)
                    below = pl.ds(pl.multiple_of(b * BLK + c * SUB, SUB), SUB)
                    here = pl.ds(pl.multiple_of(CTX + b * BLK + c * SUB, SUB), SUB)
                    for s in range(2):
                        rebuilt = tile[s * SUB:(s + 1) * SUB]
                        ext[2 * p + s, here, :] = jnp.where(z == fc, rebuilt, ext[2 * p + s, here, :])
                        ext[2 * p + s, below, :] = jnp.where(z - 1 == fc, rebuilt, ext[2 * p + s, below, :])

    a_step(2)
    lost_pieces([z])

    @pl.when(merging)
    def _():
        whole(slices.at[0:N - 1], sl_send, sl_recv).wait_recv()
        tops, totals = zip(*[stat_rows(slices[c, 16:, :]) for c in range(N)])
        top = functools.reduce(jnp.maximum, tops)
        factors = [jnp.exp(v - top) for v in tops]
        total = functools.reduce(jnp.add, [v * f for v, f in zip(totals, factors)])
        mix = functools.reduce(jnp.add, [slices[c, :16, :].astype(F32) * factors[c] for c in range(N)])
        merged[N // 2 - 1, :16, :] = mix.astype(BF16)
        merged[N // 2 - 1, 16:, :] = stat_tile(row, top, total)
        for o in range(1, N):
            me_copy(o).start()

    lost_below = z - 1 == fc

    def lower_parts(first, last):
        @pl.when(z != 0)
        def _():
            for n in range(first, last):
                a_copy(n).wait_recv()

        for n in range(first, last):
            rows = slice(n * (CTX // A_PARTS), (n + 1) * (CTX // A_PARTS))
            for i in range(4):
                ext[i, rows, :] = jnp.where(lost_below, ext[i, rows, :], lower[i, rows, :].astype(F32))

    lower_at = {3: (0, 3), 4: (3, 5), 5: (5, 7)}
    for t in range(1, HOPS + 1):
        for p in range(2):
            two_copy(t - 1, p, ring(z + 2 * t)).wait_recv()
            if t < HOPS:
                two_copy(t, p, ring(z + 2 * t)).start()
                one_copy(t, p, ring(z + 2 * t)).start()
            up_copy(t - 1, p, ring(z - t)).wait_recv()
            if t < HOPS:
                up_copy(t, p, ring(z - t)).start()
        a_step(1)
        if t in lower_at:
            lower_parts(*lower_at[t])
        for p in range(2):
            one_copy(t - 1, p, ring(z + 2 * t - 1)).wait_recv()
        lost_pieces([ring(z + 2 * t - 1), ring(z + 2 * t), ring(z - t)])
    @pl.when(merging)
    def _():
        whole(merged.at[0:N // 2 - 1], me_send, me_recv).wait_recv()

    @pl.when(jnp.logical_not(merging))
    def _():
        whole(merged, me_send, me_recv).wait_recv()

    for n in range(N // 2):
        all_mix[lax.rem(my_slice + N - n - jnp.where(merging, 1, 0), N // 2)] = merged[n, :16, :].astype(F32)
    top_alive, total_alive = stat_rows(merged[0, 16:, :])

    tops = [top_fresh, lost["top"], top_alive]
    totals = [total_fresh, lost["total"], total_alive]
    top = functools.reduce(jnp.maximum, tops)
    factors = [jnp.exp(v - top) for v in tops]
    total = functools.reduce(jnp.add, [v * f for v, f in zip(totals, factors)])
    mix = mix_fresh * factors[0] + lost_mix[...] * factors[1]
    mix = mix + jnp.concatenate([all_mix[i] for i in range(N // 2)], axis=0) * factors[2]
    att[...] = jnp.transpose(mix / total).astype(BF16)
    log_row = top + jnp.log(total)
    for n in range(8):
        turned = log_row if n == 0 else pltpu.roll(log_row, HD - 16 * n, 1)
        logs[n // 4, n % 4:n % 4 + 1, :] = turned[:, :16]

    lower_parts(7, A_PARTS)
    for seq in range(2):
        begin = jnp.int32(0)
        length = jnp.int32(0)
        for j in range(N - 1):
            size = lengths[seq, j]
            begin = begin + jnp.where(j < z - 1, size, 0)
            length = jnp.where(j == z - 1, size, length)
        offset = jnp.clip(begin - (z - 1) * CTX, 0, CTX)
        slot = iota((PIECE, HD), 0)
        for p in range(2):
            for n in range(CAP // PIECE):
                rows = ext[2 * p + seq, pl.ds(offset + n * PIECE, PIECE), :]
                rows = jnp.where(slot + n * PIECE < length, rows, 0.0)
                out[2 * p + seq, n * PIECE:(n + 1) * PIECE, :] = rows.astype(BF16)

    whole(bbuf.at[0:N - 1], b_send, b_recv).wait_send()
    whole(srow.at[0:N - 1], s_send, s_recv).wait_send()
    for p in range(2):
        whole(xbuf.at[p], x_send.at[p], x_recv.at[p]).wait_send()
    whole(msgs.at[0:N - 1], g_send, up_recv.at[0, 0]).wait_send()

    @pl.when(merging)
    def _():
        whole(slices.at[0:N // 2 - 1], sl_send, sl_recv).wait_send()
        whole(slices.at[0:N - 1], me_send, me_recv).wait_send()

    @pl.when(jnp.logical_not(merging))
    def _():
        whole(slices.at[0:N // 2], sl_send, sl_recv).wait_send()

    @pl.when(z != N - 1)
    def _():
        whole(lower, a_send, a_recv.at[0]).wait_send()


def restore(slots, *operands):
    vmem = pl.BlockSpec(memory_space=pltpu.VMEM)
    hbm = pl.BlockSpec(memory_space=pltpu.HBM)
    dma = pltpu.SemaphoreType.DMA
    return pl.pallas_call(
        functools.partial(kernel, slots),
        out_shape=(
            jax.ShapeDtypeStruct((4, CAP, HD), BF16),
            jax.ShapeDtypeStruct((HD, HD), BF16),
            jax.ShapeDtypeStruct((2, 4, 16), F32),
        ),
        in_specs=[hbm] * 8,
        out_specs=(vmem, vmem, vmem),
        scratch_shapes=[
            pltpu.VMEM((4, CTX, HD), BF16),
            pltpu.VMEM((4, CTX, HD), BF16),
            pltpu.VMEM((2, 2, BLOCKS), BF16),
            pltpu.SMEM((BLOCKS,), jnp.int32),
            pltpu.SMEM((1,), jnp.int32),
            pltpu.SMEM((2, N - 1), jnp.int32),
            pltpu.VMEM((HD, HD), BF16),
            pltpu.VMEM((16, HD), BF16),
            pltpu.VMEM((4, CTX, HD), BF16),
            pltpu.VMEM((N, slots, 2, 16, HD), BF16),
            pltpu.VMEM((N, slots, 2, 16, HD), BF16),
            pltpu.VMEM((N, 1, HD), F32),
            pltpu.VMEM((2, PACK, HD), BF16),
            pltpu.VMEM((2, MP, PACK, HD), BF16),
            pltpu.VMEM((N, 2, ROWS, HD), BF16),
            pltpu.VMEM((CTX, HD), F32),
            pltpu.VMEM((HD, HD), F32),
            pltpu.VMEM((N // 2, 32, HD), BF16),
            pltpu.VMEM((N, 32, HD), BF16),
            pltpu.VMEM((N // 2, 32, HD), BF16),
            pltpu.VMEM((N // 2, 16, HD), F32),
            pltpu.VMEM((HD, HD), F32),
            pltpu.VMEM((4, CTX + CAP, HD), F32),
            dma((8,)),
            dma, dma((A_PARTS,)),
            dma, dma, dma, dma,
            dma((2,)), dma((2,)),
            dma((HOPS, 2)), dma((HOPS, 2)), dma((HOPS, 2)),
            dma, dma, dma, dma, dma,
        ],
        compiler_params=pltpu.CompilerParams(
            collective_id=slots, has_side_effects=True, vmem_limit_bytes=56 * 1024 * 1024),
        cost_estimate=pl.CostEstimate(flops=10**8, bytes_accessed=4 * 10**6, transcendentals=2 * 10**5),
    )(*operands)


SLOTS = (2, 3, 8)


def body(kv_cache, backup_codes, backup_scales, block_shift, failed, new_lengths, queries, new_kv):
    cube = (BLOCKS,) * 3
    ids = [lax.broadcasted_iota(jnp.int32, cube, n) for n in range(3)]
    spread = [lax.broadcast_in_dim(block_shift, cube, (n,)) for n in range(3)]
    equal = (spread[0] == spread[1]) & (spread[1] == spread[2]) & (ids[0] < ids[1]) & (ids[1] < ids[2])
    triples = jnp.sum(equal.astype(jnp.int32))
    branch = (triples > 0).astype(jnp.int32) + (triples > 3).astype(jnp.int32)
    out, att, logs = lax.switch(
        branch,
        [functools.partial(restore, slots) for slots in SLOTS],
        kv_cache.reshape(4, CTX, HD),
        backup_codes.reshape(4, CTX, HD),
        backup_scales.reshape(2, 2, BLOCKS),
        block_shift,
        failed,
        new_lengths,
        queries.reshape(HD, HD),
        new_kv.reshape(16, HD),
    )
    return (
        out.reshape(2, 2, CAP, 1, HD),
        att.reshape(queries.shape),
        logs,
    )


def solution(mesh):
    return jax.shard_map(
        body,
        mesh=mesh,
        in_specs=(
            P(None, "batch", "ctx", "mp", None),
            P(None, "batch", "ctx", "mp", None),
            P(None, "batch", "ctx", "mp"),
            P(),
            P(),
            P("batch", None),
            P("batch", None, "mp", None),
            P(None, "batch", None, "mp", None),
        ),
        out_specs=(
            P(None, "batch", "ctx", "mp", None),
            P("batch", None, "mp", None),
            P("batch", None, "mp"),
        ),
        check_vma=False,
    )
```

```python
import functools
import math

import jax
import jax.numpy as jnp
from jax import lax
from jax.experimental import pallas as pl
from jax.experimental.pallas import tpu as pltpu
from jax.sharding import PartitionSpec as P

F32 = jnp.float32
BF16 = jnp.bfloat16
MESH = pl.DeviceIdType.MESH

far_below = -1e30

BLK = 128
N = 16
NB = 8
MP = 4
HD = 128
CTX = 1024
CAP = 1216
PIECE = CTX // N
ROWS = 2 * PIECE
PACK = ROWS + 16
BLOCKS = CTX // BLK
SUB = 8

HOPS = 5
A_PARTS = 8


def dot_tt(a, b):
    return lax.dot_general(a, b, (((1,), (1,)), ((), ())), preferred_element_type=F32)


def dot_sum_rows(a, b):
    return lax.dot_general(a, b, (((0,), (0,)), ((), ())), preferred_element_type=F32)


def iota(shape, dim):
    return lax.broadcasted_iota(jnp.int32, shape, dim)


def split_three(x):
    hi = x.astype(BF16).astype(F32)
    rest = x - hi
    mid = rest.astype(BF16).astype(F32)
    return hi, mid, rest - mid


def stat_tile(row, top, total):
    tile = jnp.zeros((16, HD), F32)
    for n, piece in enumerate(split_three(top) + split_three(total)):
        tile = jnp.where(row == n, piece, tile)
    return tile.astype(BF16)


def stat_rows(tile):
    tile = tile.astype(F32)
    return tile[0:1] + tile[1:2] + tile[2:3], tile[3:4] + tile[4:5] + tile[5:6]


def kernel(slots, kv_hbm, codes_hbm, scales_hbm, shift_hbm, failed_hbm, lengths_hbm, q_hbm, fresh_hbm,
           out, att, logs,
           kv, codes, scales, shift, failed, lengths, q, fresh,
           lower, bsend, bbuf, srow, xsend, xbuf, msgs, score, own_mix, sent_mix, slices, merged, all_mix, lost_mix, ext,
           in_sem, a_send, a_recv, b_send, b_recv, s_send, s_recv, x_send, x_recv,
           one_recv, two_recv, up_recv, g_send, sl_send, sl_recv, me_send, me_recv):
    z = lax.axis_index("ctx")
    g = lax.axis_index("batch")
    k = lax.axis_index("mp")

    fetch = [
        pltpu.make_async_copy(source, target, in_sem.at[n])
        for n, (source, target) in enumerate((
            (codes_hbm, codes), (failed_hbm, failed), (shift_hbm, shift), (scales_hbm, scales),
            (kv_hbm, kv), (q_hbm, q), (fresh_hbm, fresh), (lengths_hbm, lengths)))
    ]
    for copy in fetch:
        copy.start()

    def ring(c):
        return lax.rem(c + 2 * N, N)

    g_to, g_from = lax.rem(g + NB - 1, NB), lax.rem(g + 1, NB)

    barrier = pltpu.get_barrier_semaphore()
    for o in range(1, N):
        pl.semaphore_signal(barrier, inc=1, device_id=(ring(z + o), g, k), device_id_type=MESH)
    for j in range(MP):
        pl.semaphore_signal(barrier, inc=1, device_id=(z, g_to, j), device_id_type=MESH)
        pl.semaphore_signal(barrier, inc=1, device_id=(z, g_from, j), device_id_type=MESH)

    for copy in fetch[:4]:
        copy.wait()
    fc = lax.rem(failed[0], N)
    lane = iota((16, HD), 1)
    row = iota((16, HD), 0)

    shifts = [shift[b] for b in range(BLOCKS)]
    holder = [lax.rem(fc + v, N) for v in shifts]
    rank = []
    for b in range(BLOCKS):
        before = jnp.int32(0)
        for e in range(b):
            before = before + jnp.where(shifts[e] == shifts[b], 1, 0)
        rank.append(jnp.minimum(before, slots - 1))
    def chosen(b, h, j):
        return (holder[b] == h) & (rank[b] == j)

    for j in range(slots):
        for p in range(2):
            pair = []
            for s in range(2):
                block = codes[2 * p + s, j * BLK:(j + 1) * BLK, :]
                for b in range(j + 1, BLOCKS):
                    block = jnp.where(chosen(b, z, j), codes[2 * p + s, b * BLK:(b + 1) * BLK, :], block)
                pair.append(block.astype(F32))
            for c in range(N):
                part = slice(c * SUB, (c + 1) * SUB)
                bsend[c, j, p] = jnp.concatenate([pair[0][part], pair[1][part]], axis=0).astype(BF16)
    line = jnp.zeros((1, HD), F32)
    for p in range(2):
        both = scales[p].astype(F32)
        for s in range(2):
            wide = jnp.concatenate([both[s:s + 1], jnp.zeros((1, HD - BLOCKS), F32)], axis=1)
            at = (2 * p + s) * BLOCKS
            line = line + (pltpu.roll(wide, at, 1) if at else wide)
    srow[N - 1] = line
    bbuf[N - 1] = bsend[z]

    def peer_copy(o, source, target, send, recv):
        return pltpu.make_async_remote_copy(
            src_ref=source, dst_ref=target, send_sem=send, recv_sem=recv,
            device_id=(ring(z + o), g, k), device_id_type=MESH)

    def b_copy(o):
        return peer_copy(o, bsend.at[ring(z + o)], bbuf.at[o - 1], b_send, b_recv)

    def s_copy(o):
        return peer_copy(o, srow.at[N - 1], srow.at[o - 1], s_send, s_recv)

    def sl_copy(o):
        return peer_copy(o, sent_mix.at[ring(z + o) // 2], slices.at[o - 1], sl_send, sl_recv)

    def me_copy(o):
        return peer_copy(o, merged.at[N // 2 - 1], merged.at[(o - 1) // 2], me_send, me_recv)

    def whole(ref, send, recv):
        return peer_copy(1, ref, ref, send, recv)

    even, odd = range(2, N, 2), range(1, N, 2)
    merging = lax.rem(z, 2) == 0
    my_slice = z // 2

    order = [8, 7, 9, 6, 10, 5, 11, 4, 12, 3, 13, 2, 14, 1, 15]
    pl.semaphore_wait(barrier, N - 1 + 2 * MP)
    for o in order:
        b_copy(o).start()
        s_copy(o).start()

    def a_copy(n):
        rows = pl.ds(pl.multiple_of(n * (CTX // A_PARTS), CTX // A_PARTS), CTX // A_PARTS)
        return pltpu.make_async_remote_copy(
            src_ref=kv.at[:, rows, :], dst_ref=lower.at[:, rows, :], send_sem=a_send, recv_sem=a_recv.at[n],
            device_id=(ring(z + 1), g, k), device_id_type=MESH)

    a_started = [0]

    def a_step(count):
        first = a_started[0]
        last = min(first + count, A_PARTS)
        a_started[0] = last

        @pl.when(z != N - 1)
        def _():
            for n in range(first, last):
                a_copy(n).start()

    for copy in fetch[4:]:
        copy.wait()

    half = iota((HD, HD), 0) < HD // 2
    queries = q[...]
    zero = jnp.zeros((HD, HD), BF16)
    q0, q1 = jnp.where(half, queries, zero), jnp.where(half, zero, queries)
    first_half = iota((1, HD), 1) < HD // 2
    scaling = 1.0 / math.sqrt(HD)
    alive = z != fc
    CH = 256

    def rows_of(n, size):
        return pl.ds(pl.multiple_of(n * size, size), size)

    def score_step(n, top):
        rows = rows_of(n, CH)
        s = (dot_tt(kv[0, rows, :], q0) + dot_tt(kv[1, rows, :], q1)) * scaling
        s = jnp.where(alive, s, far_below)
        score[rows, :] = s
        return jnp.maximum(top, jnp.max(s, axis=0, keepdims=True))

    top_own = lax.fori_loop(0, CTX // CH, score_step, jnp.full((1, HD), far_below, F32))
    own_mix[...] = jnp.zeros((HD, HD), F32)

    def weigh_step(n, total):
        rows = rows_of(n, CH)
        w = jnp.where(alive, jnp.exp(score[rows, :] - top_own), 0.0)
        w0 = jnp.where(first_half, w, 0.0).astype(BF16)
        w1 = jnp.where(first_half, 0.0, w).astype(BF16)
        own_mix[...] += dot_sum_rows(kv[2, rows, :], w0) + dot_sum_rows(kv[3, rows, :], w1)
        return total + jnp.sum(w, axis=0, keepdims=True)

    total_own = lax.fori_loop(0, CTX // CH, weigh_step, jnp.zeros((1, HD), F32))
    tile = stat_tile(row, top_own, total_own)
    for i in range(N // 2):
        sent_mix[i, :16, :] = own_mix[16 * i:16 * i + 16, :].astype(BF16)
        sent_mix[i, 16:, :] = tile
    slices[N - 1] = sent_mix[my_slice]

    fresh_rows = fresh[...]
    s = dot_tt(fresh_rows, queries) * scaling
    usable = (row < 8) & (row // 4 == lane // 64) & (lax.rem(row, 4) <= lax.rem(lane, 64) // 16)
    s = jnp.where(usable, s, far_below)
    top_fresh = jnp.max(s, axis=0, keepdims=True)
    w = jnp.where(usable, jnp.exp(s - top_fresh), 0.0)
    total_fresh = jnp.sum(w, axis=0, keepdims=True)
    w = jnp.concatenate([jnp.zeros((8, HD), F32), w[:8]], axis=0).astype(BF16)
    mix_fresh = dot_sum_rows(fresh_rows, w)

    shared = iota((HD, HD), 0) & iota((HD, HD), 1)
    shared = shared ^ (shared >> 4)
    shared = shared ^ (shared >> 2)
    shared = (shared ^ (shared >> 1)) & 1
    signs = (1 - 2 * shared).astype(F32).astype(BF16)

    def widen_step(n, carry):
        for i in range(4):
            ext[i, pl.ds(pl.multiple_of(CTX + n * PIECE, PIECE), PIECE), :] = kv[i, rows_of(n, PIECE), :].astype(F32)
        return carry

    lax.fori_loop(0, N, widen_step, 0)
    for i in range(4):
        ext[i, 2 * CTX:, :] = jnp.zeros((CAP - CTX, HD), F32)

    whole(srow.at[0:N - 1], s_send, s_recv).wait_recv()
    away = [ring(z - h) for h in holder]
    away = [jnp.where(v == 0, N - 1, v - 1) for v in away]
    tiles = [jnp.zeros((16, HD), F32) for _ in range(2)]
    for b in range(BLOCKS):
        line = srow[0]
        for h in range(1, N):
            line = jnp.where(away[b] == h, srow[h], line)
        for p in range(2):
            for s in range(2):
                at = (2 * p + s) * BLOCKS + b
                tiles[p] = jnp.where(row == 2 * b + s, line[:, at:at + 1], tiles[p])

    whole(bbuf.at[0:N - 1], b_send, b_recv).wait_recv()
    a_step(1)

    def x_copy(j, p, slot):
        return pltpu.make_async_remote_copy(
            src_ref=xsend.at[p], dst_ref=xbuf.at[p, slot],
            send_sem=x_send.at[p], recv_sem=x_recv.at[p],
            device_id=(z, g_to, j), device_id_type=MESH)

    for p in range(2):
        for b in range(BLOCKS):
            tile = bbuf[0, 0, p]
            for h in range(N):
                for j in range(min(slots, b + 1)):
                    if h + j > 0:
                        tile = jnp.where((away[b] == h) & (rank[b] == j), bbuf[h, j, p], tile)
            xsend[p, b * 16:(b + 1) * 16, :] = tile
        xsend[p, ROWS:, :] = tiles[p].astype(BF16)
        for j in range(MP):
            x_copy(j, p, k).start()
    @pl.when(merging)
    def _():
        for o in even:
            sl_copy(o).start()

    @pl.when(jnp.logical_not(merging))
    def _():
        for o in odd:
            sl_copy(o).start()

    a_step(2)

    def one_copy(t, p, piece):
        return pltpu.make_async_remote_copy(
            src_ref=msgs.at[piece, p], dst_ref=msgs.at[piece, p], send_sem=g_send, recv_sem=one_recv.at[t, p],
            device_id=(ring(z - 1), g, k), device_id_type=MESH)

    def two_copy(t, p, piece):
        return pltpu.make_async_remote_copy(
            src_ref=msgs.at[piece, p], dst_ref=msgs.at[piece, p], send_sem=g_send, recv_sem=two_recv.at[t, p],
            device_id=(ring(z - 2), g, k), device_id_type=MESH)

    def up_copy(t, p, piece):
        return pltpu.make_async_remote_copy(
            src_ref=msgs.at[piece, p], dst_ref=msgs.at[piece, p], send_sem=g_send, recv_sem=up_recv.at[t, p],
            device_id=(ring(z + 1), g, k), device_id_type=MESH)

    norm = 1.0 / math.sqrt(MP * HD)
    for p in range(2):
        mixed = None
        whole(xbuf.at[p], x_send.at[p], x_recv.at[p]).wait_recv()
        for j in range(MP):
            common = k & j
            odd = (common ^ (common >> 1)) & 1
            coef = jnp.where(odd == 1, -norm, norm).astype(F32)
            tile = xbuf[p, j, ROWS:, :].astype(F32)
            wide = jnp.concatenate([jnp.broadcast_to(tile[r:r + 1], (SUB, HD)) for r in range(16)], axis=0)
            term = jnp.dot(xbuf[p, j, :ROWS, :], signs, preferred_element_type=F32) * wide * coef
            mixed = term if j == 0 else mixed + term
        msgs[z, p] = mixed.astype(BF16)
        two_copy(0, p, z).start()
        up_copy(0, p, z).start()
        one_copy(0, p, z).start()

    def lost_pieces(pieces, lost):
        count = len(pieces)
        keys = jnp.concatenate([msgs[c, 0] for c in pieces], axis=0)
        values = jnp.concatenate([msgs[c, 1] for c in pieces], axis=0)
        matching = ((iota((ROWS * count, HD), 0) // SUB) & 1) == iota((ROWS * count, HD), 1) // (HD // 2)
        s = jnp.where(matching, dot_tt(keys, queries) * scaling, far_below)
        top = jnp.max(s, axis=0, keepdims=True)
        if lost:
            top = jnp.maximum(top, lost[0])
        w = jnp.where(matching, jnp.exp(s - top), 0.0)
        total = jnp.sum(w, axis=0, keepdims=True)
        mix = dot_sum_rows(values, w.astype(BF16))
        if lost:
            factor = jnp.exp(lost[0] - top)
            total = total + lost[1] * factor
            mix = mix + lost_mix[...] * factor
        lost_mix[...] = mix

        def place(b, carry):
            for c in pieces:
                below = pl.ds(pl.multiple_of(b * BLK + c * SUB, SUB), SUB)
                here = pl.ds(pl.multiple_of(CTX + b * BLK + c * SUB, SUB), SUB)
                for p in range(2):
                    tile = msgs[c, p, rows_of(b, 16), :].astype(F32)
                    for s in range(2):
                        rebuilt = tile[s * SUB:(s + 1) * SUB]
                        ext[2 * p + s, here, :] = jnp.where(z == fc, rebuilt, ext[2 * p + s, here, :])
                        ext[2 * p + s, below, :] = jnp.where(z - 1 == fc, rebuilt, ext[2 * p + s, below, :])
            return carry

        lax.fori_loop(0, BLOCKS, place, 0)
        return top, total

    a_step(1)
    first_lost = lost_pieces([z], None)

    @pl.when(merging)
    def _():
        whole(slices.at[0:N - 1], sl_send, sl_recv).wait_recv()
        tops, totals = zip(*[stat_rows(slices[c, 16:, :]) for c in range(N)])
        top = functools.reduce(jnp.maximum, tops)
        factors = [jnp.exp(v - top) for v in tops]
        total = functools.reduce(jnp.add, [v * f for v, f in zip(totals, factors)])
        mix = functools.reduce(jnp.add, [slices[c, :16, :].astype(F32) * factors[c] for c in range(N)])
        merged[N // 2 - 1, :16, :] = mix.astype(BF16)
        merged[N // 2 - 1, 16:, :] = stat_tile(row, top, total)
        for o in range(1, N):
            me_copy(o).start()

    lost_below = z - 1 == fc

    def lower_part(n):
        @pl.when(z != 0)
        def _():
            a_copy(n).wait_recv()

        rows = rows_of(n, CTX // A_PARTS)
        for i in range(4):
            ext[i, rows, :] = jnp.where(lost_below, ext[i, rows, :], lower[i, rows, :].astype(F32))

    def hop(t, lost):
        for p in range(2):
            two_copy(t - 1, p, ring(z + 2 * t)).wait_recv()

            @pl.when(t < HOPS)
            def _():
                two_copy(t, p, ring(z + 2 * t)).start()
                one_copy(t, p, ring(z + 2 * t)).start()

        for p in range(2):
            up_copy(t - 1, p, ring(z - t)).wait_recv()

            @pl.when(t < HOPS)
            def _():
                up_copy(t, p, ring(z - t)).start()

        @pl.when((t <= A_PARTS - 4) & (z != N - 1))
        def _():
            a_copy(3 + t).start()

        @pl.when(t >= 3)
        def _():
            for u in range(2):
                lower_part(2 * (t - 3) + u)

        for p in range(2):
            one_copy(t - 1, p, ring(z + 2 * t - 1)).wait_recv()
        return lost_pieces([ring(z + 2 * t - 1), ring(z + 2 * t), ring(z - t)], lost)

    top_lost, total_lost = lax.fori_loop(1, HOPS + 1, hop, first_lost)
    @pl.when(merging)
    def _():
        whole(merged.at[0:N // 2 - 1], me_send, me_recv).wait_recv()

    @pl.when(jnp.logical_not(merging))
    def _():
        whole(merged, me_send, me_recv).wait_recv()

    for n in range(N // 2):
        all_mix[lax.rem(my_slice + N - n - jnp.where(merging, 1, 0), N // 2)] = merged[n, :16, :].astype(F32)
    top_alive, total_alive = stat_rows(merged[0, 16:, :])

    tops = [top_fresh, top_lost, top_alive]
    totals = [total_fresh, total_lost, total_alive]
    top = functools.reduce(jnp.maximum, tops)
    factors = [jnp.exp(v - top) for v in tops]
    total = functools.reduce(jnp.add, [v * f for v, f in zip(totals, factors)])
    mix = mix_fresh * factors[0] + lost_mix[...] * factors[1]
    mix = mix + jnp.concatenate([all_mix[i] for i in range(N // 2)], axis=0) * factors[2]
    att[...] = jnp.transpose(mix / total).astype(BF16)
    log_row = top + jnp.log(total)
    for n in range(8):
        turned = log_row if n == 0 else pltpu.roll(log_row, HD - 16 * n, 1)
        logs[n // 4, n % 4:n % 4 + 1, :] = turned[:, :16]

    for n in range(6, A_PARTS):
        lower_part(n)
    offsets, filled = [], []
    for seq in range(2):
        begin = jnp.int32(0)
        length = jnp.int32(0)
        for j in range(N - 1):
            size = lengths[seq, j]
            begin = begin + jnp.where(j < z - 1, size, 0)
            length = jnp.where(j == z - 1, size, length)
        offsets.append(jnp.clip(begin - (z - 1) * CTX, 0, CTX))
        filled.append(length)
    slot = iota((PIECE, HD), 0)

    def final_step(n, carry):
        for p in range(2):
            for seq in range(2):
                rows = ext[2 * p + seq, pl.ds(offsets[seq] + n * PIECE, PIECE), :]
                rows = jnp.where(slot < filled[seq] - n * PIECE, rows, 0.0)
                out[2 * p + seq, rows_of(n, PIECE), :] = rows.astype(BF16)
        return carry

    lax.fori_loop(0, CAP // PIECE, final_step, 0)

    whole(bbuf.at[0:N - 1], b_send, b_recv).wait_send()
    whole(srow.at[0:N - 1], s_send, s_recv).wait_send()
    for p in range(2):
        whole(xbuf.at[p], x_send.at[p], x_recv.at[p]).wait_send()
    whole(msgs.at[0:N - 1], g_send, up_recv.at[0, 0]).wait_send()

    @pl.when(merging)
    def _():
        whole(slices.at[0:N // 2 - 1], sl_send, sl_recv).wait_send()
        whole(slices.at[0:N - 1], me_send, me_recv).wait_send()

    @pl.when(jnp.logical_not(merging))
    def _():
        whole(slices.at[0:N // 2], sl_send, sl_recv).wait_send()

    @pl.when(z != N - 1)
    def _():
        whole(lower, a_send, a_recv.at[0]).wait_send()


def restore(slots, *operands):
    vmem = pl.BlockSpec(memory_space=pltpu.VMEM)
    hbm = pl.BlockSpec(memory_space=pltpu.HBM)
    dma = pltpu.SemaphoreType.DMA
    return pl.pallas_call(
        functools.partial(kernel, slots),
        out_shape=(
            jax.ShapeDtypeStruct((4, CAP, HD), BF16),
            jax.ShapeDtypeStruct((HD, HD), BF16),
            jax.ShapeDtypeStruct((2, 4, 16), F32),
        ),
        in_specs=[hbm] * 8,
        out_specs=(vmem, vmem, vmem),
        scratch_shapes=[
            pltpu.VMEM((4, CTX, HD), BF16),
            pltpu.VMEM((4, CTX, HD), BF16),
            pltpu.VMEM((2, 2, BLOCKS), BF16),
            pltpu.SMEM((BLOCKS,), jnp.int32),
            pltpu.SMEM((1,), jnp.int32),
            pltpu.SMEM((2, N - 1), jnp.int32),
            pltpu.VMEM((HD, HD), BF16),
            pltpu.VMEM((16, HD), BF16),
            pltpu.VMEM((4, CTX, HD), BF16),
            pltpu.VMEM((N, slots, 2, 16, HD), BF16),
            pltpu.VMEM((N, slots, 2, 16, HD), BF16),
            pltpu.VMEM((N, 1, HD), F32),
            pltpu.VMEM((2, PACK, HD), BF16),
            pltpu.VMEM((2, MP, PACK, HD), BF16),
            pltpu.VMEM((N, 2, ROWS, HD), BF16),
            pltpu.VMEM((CTX, HD), F32),
            pltpu.VMEM((HD, HD), F32),
            pltpu.VMEM((N // 2, 32, HD), BF16),
            pltpu.VMEM((N, 32, HD), BF16),
            pltpu.VMEM((N // 2, 32, HD), BF16),
            pltpu.VMEM((N // 2, 16, HD), F32),
            pltpu.VMEM((HD, HD), F32),
            pltpu.VMEM((4, CTX + CAP, HD), F32),
            dma((8,)),
            dma, dma((A_PARTS,)),
            dma, dma, dma, dma,
            dma((2,)), dma((2,)),
            dma((HOPS, 2)), dma((HOPS, 2)), dma((HOPS, 2)),
            dma, dma, dma, dma, dma,
        ],
        compiler_params=pltpu.CompilerParams(
            collective_id=slots, has_side_effects=True, vmem_limit_bytes=56 * 1024 * 1024),
        cost_estimate=pl.CostEstimate(flops=10**8, bytes_accessed=4 * 10**6, transcendentals=2 * 10**5),
    )(*operands)


SLOTS = (2, 3, 8)


def body(kv_cache, backup_codes, backup_scales, block_shift, failed, new_lengths, queries, new_kv):
    tens = jnp.uint32(1) << (4 * (block_shift & 7)).astype(jnp.uint32)
    low = jnp.sum(jnp.where(block_shift < 8, tens, 0), dtype=jnp.uint32)
    high = jnp.sum(jnp.where(block_shift < 8, 0, tens), dtype=jnp.uint32)
    tops = jnp.uint32(0x88888888)
    three = ((low + jnp.uint32(0x55555555)) | (high + jnp.uint32(0x55555555))) & tops
    four = ((low + jnp.uint32(0x44444444)) | (high + jnp.uint32(0x44444444))) & tops
    branch = (three != 0).astype(jnp.int32) + (four != 0).astype(jnp.int32)
    out, att, logs = lax.switch(
        branch,
        [functools.partial(restore, slots) for slots in SLOTS],
        kv_cache.reshape(4, CTX, HD),
        backup_codes.reshape(4, CTX, HD),
        backup_scales.reshape(2, 2, BLOCKS),
        block_shift,
        failed,
        new_lengths,
        queries.reshape(HD, HD),
        new_kv.reshape(16, HD),
    )
    return (
        out.reshape(2, 2, CAP, 1, HD),
        att.reshape(queries.shape),
        logs,
    )


def solution(mesh):
    return jax.shard_map(
        body,
        mesh=mesh,
        in_specs=(
            P(None, "batch", "ctx", "mp", None),
            P(None, "batch", "ctx", "mp", None),
            P(None, "batch", "ctx", "mp"),
            P(),
            P(),
            P("batch", None),
            P("batch", None, "mp", None),
            P(None, "batch", None, "mp", None),
        ),
        out_specs=(
            P(None, "batch", "ctx", "mp", None),
            P("batch", None, "mp", None),
            P("batch", None, "mp"),
        ),
        check_vma=False,
    )
```
